128 devices in a mesh: wide: 32 (over z, x_hi, y), narrow: 4 (over x_lo, core).
Axes of the slice: x: 4 (x_hi: 2, x_lo: 2; x = x_hi * 2 + x_lo), y: 4, z: 4, core: 2. Of those that a mesh axis runs over, the one named last changes fastest.
Arguments:
- amplitudes: float32 [2, 4, 1024, 1024], P(None, None, 'wide', 'narrow'), may hold values from -2 to 2
- cycle_amps: bfloat16 [2, 64, 1024, 1024], P(None, None, 'wide', 'narrow'), may hold values from -6 to 6
- cycle_ints: bfloat16 [64, 1024, 4, 1024], P(None, 'wide'), may hold values from -0.25 to 0.25
- ladder_ints: bfloat16 [64, 4, 1024, 1024], P(None, None, 'wide', 'narrow'), may hold values from -0.01171875 to 0.01171875
- integrals: float32 [2, 4, 1024, 1024], P(None, None, 'wide', 'narrow'), may hold values from -13 to 13
- history: float32 [4, 2, 4, 1024, 1024], P(None, None, None, 'wide', 'narrow'), may hold values from -22 to 22
- vir_energy: float32 [1024], replicated, may hold values from 0.5 to 3
- occ_first: float32 [2], replicated, may hold values from -1.5 to -0.3
- occ_second: float32 [4], replicated, may hold values from -1.2 to -0.2
Outputs:
- updated: float32 [2, 4, 1024, 1024], P(None, None, 'wide', 'narrow')
- residual: float32 [2, 4, 1024, 1024], P(None, None, 'wide', 'narrow')
- energy: float32 [1], replicated
- intersections: float32 [5], replicated
The draws below stay inside these ranges and needn't reach their ends.
All inputs are finite; a program needn't handle non-finite values.
Results may differ from the reference program's by a relative error of at most 0.0003.
Values sent between devices are 32-bit elements; how exact they have to be, the bound alone decides.
A program may use at most 128 MiB of HBM per device.

```python
import math
import jax
import jax.numpy as jnp
from jax import lax

V = 1024
NI = 2
NJ = 4
NK = 64
AWD = 2
BWD = 1
NH = 4
AL = 64
BL = 4
N_WIDE = 32
N_NARROW = 4


def shared_field(key, spread):
    rough_part = jnp.clip(jax.random.normal(jax.random.fold_in(key, 11), (NI, NJ, V, V), jnp.float32), -4.0, 4.0)
    log_spread = math.log(spread)
    row_scale = jnp.exp(jax.random.uniform(jax.random.fold_in(key, 12), (V,), jnp.float32, -log_spread, log_spread))
    col_scale = jnp.exp(jax.random.uniform(jax.random.fold_in(key, 13), (V,), jnp.float32, -log_spread, log_spread))
    return rough_part * row_scale[None, None, :, None] * col_scale[None, None, None, :]


def draw_integrals(key, part):
    spread = 1.0
    common = shared_field(key, spread)
    return common


def draw_history(key, part):
    spread = 1.0
    common = shared_field(key, spread)
    key = jax.random.fold_in(key, 5)
    sign_flip = jax.random.rademacher(jax.random.fold_in(key, 1), (NH,), jnp.int32).astype(jnp.float32)
    weights = sign_flip * jax.random.uniform(jax.random.fold_in(key, 2), (NH,), jnp.float32, 0.4, 1.5)
    jitter = 0.5 * jnp.clip(jax.random.normal(jax.random.fold_in(key, 4), (NH, NI, NJ, V, V), jnp.float32), -4.0, 4.0)
    return weights[:, None, None, None, None] * common[None] + jitter


def raised(result, key, source, target, parts, factor):
    def block_of(dim):
        return (jnp.arange(result.shape[dim]) // (result.shape[dim] // parts)).reshape((-1,) + (1,) * (result.ndim - 1 - dim))

    one_side = jax.random.permutation(key, parts)[block_of(target)]
    second = (block_of(target) + parts // 2) % parts
    return jnp.where((block_of(source) == one_side) | (block_of(source) == second), factor * result, result)


def shard_levels(own_key, shape, pieces, smallest, largest):
    gain, own = 1.0, jax.random.fold_in(own_key, 6)
    for dim, parts in pieces:
        heights = jnp.exp(jax.random.uniform(jax.random.fold_in(own, dim), (parts,), jnp.float32, smallest / len(pieces), largest / len(pieces)))
        gain = gain * jnp.repeat(heights, shape[dim] // parts).reshape([-1 if axis == dim else 1 for axis in range(len(shape))])
    return gain


def gaussian(own_key, dims, scale, bound, pieces=(), kind=jnp.bfloat16):
    loudness = shard_levels(own_key, dims, pieces, -0.22, 0.18) if pieces else 1.0
    entries = jax.random.normal(own_key, dims, jnp.float32) * scale * loudness
    return jnp.minimum(jnp.maximum(entries, -bound), bound).astype(kind)


def gaussian_with(own_key, extent, deviation, reach, cuts, heavy, kind=jnp.bfloat16):
    result = deviation * jax.random.normal(own_key, extent, jnp.float32)
    if cuts:
        result = result * shard_levels(own_key, extent, cuts, -0.22, 0.18)
    return jnp.clip(raised(result, jax.random.fold_in(own_key, 3), *heavy), -reach, reach).astype(kind)


def setup_inputs(seed: int = 0) -> dict:
    keys = jax.random.split(jax.random.key(seed), 10)
    amplitudes = gaussian(keys[0], (NI, NJ, V, V), 0.3, 2.0, ((2, 32), (3, 4)), jnp.float32)
    cycle_amps = gaussian(keys[1], (NI, NK, V, V), 1.0, 6.0, ((2, 32), (3, 4)))
    cycle_ints = gaussian_with(keys[2], (NK, V, NJ, V), (NK * V // 36) ** -0.5, 0.25, ((1, 32),), (1, 3, 32, 2.75))
    ladder_ints = gaussian_with(keys[3], (AL, BL, V, V), (V * V) ** -0.5, 0.01171875, ((2, 32), (3, 4)), (2, 0, 32, 2.75))
    integrals = draw_integrals(jax.random.fold_in(keys[9], 71), 0)
    history = draw_history(jax.random.fold_in(keys[9], 71), 0)
    vir_energy = jnp.clip(jax.random.uniform(keys[6], (V,), jnp.float32, 0.5, 3.0), 0.5, 3.0)
    occ_first = jnp.clip(jax.random.uniform(keys[7], (NI,), jnp.float32, -1.5, -0.3), -1.5, -0.3)
    occ_second = jnp.clip(jax.random.uniform(keys[8], (NJ,), jnp.float32, -1.2, -0.2), -1.2, -0.2)
    return dict(amplitudes=amplitudes, cycle_amps=cycle_amps, cycle_ints=cycle_ints, ladder_ints=ladder_ints, integrals=integrals, history=history, vir_energy=vir_energy, occ_first=occ_first, occ_second=occ_second)


def reference(amplitudes, cycle_amps, cycle_ints, ladder_ints, integrals, history, vir_energy, occ_first, occ_second):
    cycle_term = jnp.einsum("ikca,kcjb->ijba", cycle_amps.astype(jnp.float32), cycle_ints.astype(jnp.float32))
    rounded = amplitudes.astype(jnp.bfloat16).reshape(NI * NJ, V * V)
    flat_ints = ladder_ints.reshape(AL * BL, V * V)
    ladder = lax.dot_general(rounded, flat_ints, (((1,), (1,)), ((), ())), preferred_element_type=jnp.float32)
    ladder = ladder.reshape(NI, NJ, AL, BL)
    span_rows = jnp.arange(AL, dtype=jnp.int32)
    span_cols = jnp.arange(BL, dtype=jnp.int32)
    ladder_rows = (span_rows // AWD) * (V // N_WIDE) + span_rows % AWD
    ladder_cols = (span_cols // BWD) * (V // N_NARROW) + span_cols % BWD
    placed = jnp.zeros((NI, NJ, V, V), jnp.float32).at[:, :, ladder_rows[:, None], ladder_cols[None, :]].set(ladder)
    denominator = (vir_energy[None, None, :, None] + vir_energy[None, None, None, :]
                   - occ_first[:, None, None, None] - occ_second[None, :, None, None])
    residual = integrals + cycle_term + placed - denominator * amplitudes
    updated = amplitudes + residual / denominator
    cell_count = float(NI * NJ * V * V)
    energy = (jnp.sum(updated * integrals) / cell_count).reshape(1)
    history_part = jnp.einsum("hijab,ijab->h", history, residual, precision=lax.Precision.HIGHEST)
    intersections = jnp.concatenate([history_part, jnp.sum(residual * residual)[None]]) / cell_count
    return updated, residual, energy, intersections
```

```python
import jax
import jax.numpy as jnp
from jax import lax
from jax.experimental import pallas as pl
from jax.experimental.pallas import tpu as pltpu
from jax.sharding import PartitionSpec as P

NI = 2
NJ = 4
DEPTH = 2048
MESH = pl.DeviceIdType.MESH
CHUNKS = (2, 1, 3, 0)
F32 = jnp.float32


def kernel(
    amp_hbm, u_hbm, m_hbm, lad_hbm, itg_hbm, his_hbm, vir_hbm, of_ref, os_ref,
    upd_hbm, res_hbm, ene_ref, int_ref,
    mbuf, ubuf, wbuf, part, r1, rx, r3,
    lbuf, lgrp, lsum, lrecv_n, lrecv_z, lrecv_x, lrecv_y,
    amp, itg, his, vir, upd, res, sc_x, sc_y, sc_z,
    lsem, s1, q1, sx, qx, s3, q3, sl, ql, ss, qs,
):
    wide = lax.axis_index("wide")
    narrow = lax.axis_index("narrow")
    z = wide // 8
    xh = lax.rem(wide // 4, 2)
    y = lax.rem(wide, 4)
    xl = narrow // 2
    core = lax.rem(narrow, 2)
    xpos = xh * 2 + xl

    def at(z_, y_, x_, core_):
        return {
            "wide": lax.rem(z_, 4) * 8 + lax.rem(x_, 4) // 2 * 4 + lax.rem(y_, 4),
            "narrow": lax.rem(x_, 2) * 2 + lax.rem(core_, 2),
        }

    def along(axis, delta):
        if axis == "z":
            return at(z + delta, y, xpos, core)
        if axis == "y":
            return at(z, y + delta, xpos, core)
        return at(z, y, xpos + delta, core)

    barrier = pltpu.get_barrier_semaphore()
    greeted = [along("z", d) for d in (1, 2, 3)] + [along("y", d) for d in (1, 2, 3)]
    greeted += [at(z, y, xpos + d // 2, core + d % 2) for d in range(1, 8)]
    for device in greeted:
        pl.semaphore_signal(barrier, inc=1, device_id=device, device_id_type=MESH)

    loads = {}

    def load(name, src, dst, n):
        loads[name] = pltpu.make_async_copy(src, dst, lsem.at[n])
        loads[name].start()

    def columns(c):
        zc = lax.rem(z + CHUNKS[c], 4)
        return pl.ds(pl.multiple_of(zc * 256, 256), 256)

    load("u", u_hbm, ubuf, 0)
    for c in range(4):
        load(("m", c), m_hbm.at[:, :, columns(c)], mbuf.at[c], 1 + c)
    load("amp", amp_hbm, amp, 5)
    load("lad", lad_hbm, lbuf, 6)
    load("itg", itg_hbm, itg, 7)
    load("his", his_hbm, his, 8)
    load("vir", vir_hbm, vir, 9)

    sends = []
    posted = {}

    def send(key, src, dst, ssem, rsem, device):
        copy = pltpu.make_async_remote_copy(
            src_ref=src, dst_ref=dst, send_sem=ssem, recv_sem=rsem, device_id=device, device_id_type=MESH
        )
        copy.start()
        sends.append(copy)
        posted[key] = copy

    ring_axis = ("z", "y")
    ring_pos = (z, y)
    chunk_pos = (y, z)

    def places(cls, ring_offset, c):
        ring = lax.rem(ring_pos[cls] + ring_offset, 4)
        chunk = lax.rem(chunk_pos[cls] + CHUNKS[c], 4)
        return (ring, chunk) if cls == 0 else (chunk, ring)

    def whole(cls, i, ring_offset, c):
        zp, yp = places(cls, ring_offset, c)
        return part.at[pl.ds(2 * cls, 2), i, zp, :, yp]

    def own_x(cls, i, c):
        zp, yp = places(cls, 0, c)
        return part.at[pl.ds(2 * cls, 2), i, zp, xh, yp]

    def ring_send(cls, kind, c, i, ring_offset, step):
        send(("r", cls, kind, c), whole(cls, i, ring_offset, c), r1.at[cls, kind, c],
             s1.at[cls, kind, c], q1.at[cls, kind, c], along(ring_axis[cls], step))

    def m1(cls, c):
        ring_send(cls, 0, c, 0, 2, 1)
        ring_send(cls, 1, c, 1, 2, 3)

    def m2_up(cls, c):
        ring_send(cls, 2, c, 1, 1, 1)

    def m2_down(cls, c):
        ring_send(cls, 3, c, 0, 3, 3)

    def m3_up(cls, c):
        posted["r", cls, 0, c].wait_recv()
        ref = whole(cls, 0, 1, c)
        ref[...] += r1[cls, 0, c]
        ring_send(cls, 4, c, 0, 1, 1)

    def m3_down(cls, c):
        posted["r", cls, 1, c].wait_recv()
        ref = whole(cls, 1, 3, c)
        ref[...] += r1[cls, 1, c]
        ring_send(cls, 5, c, 1, 3, 3)

    def ring_end(cls, c):
        for kind in (2, 3, 4, 5):
            posted["r", cls, kind, c].wait_recv()
        first = whole(cls, 0, 0, c)
        first[...] += r1[cls, 4, c] + r1[cls, 3, c]
        second = whole(cls, 1, 0, c)
        second[...] += r1[cls, 2, c] + r1[cls, 5, c]
        zp, yp = places(cls, 0, c)
        send(("x", cls, c), part.at[pl.ds(2 * cls, 2), :, zp, 1 - xh, yp], rx.at[cls, c],
             sx.at[cls, c], qx.at[cls, c], along("x", 2))

    def pair_end(cls, c):
        posted["x", cls, c].wait_recv()
        zp, yp = places(cls, 0, c)
        ref = part.at[pl.ds(2 * cls, 2), :, zp, xh, yp]
        ref[...] += rx[cls, c]

    def late_send(cls, kind, c, i, step):
        send(("l", cls, kind), own_x(cls, i, c), r3.at[cls, kind], s3.at[cls, kind], q3.at[cls, kind],
             along(ring_axis[1 - cls], step))

    def late0(cls):
        pair_end(cls, 0)
        late_send(cls, 0, 0, 0, 1)
        late_send(cls, 1, 0, 1, 3)

    def late1(cls):
        pair_end(cls, 1)
        late_send(cls, 2, 1, 1, 1)
        posted["l", cls, 0].wait_recv()
        ref = own_x(cls, 0, 1)
        ref[...] += r3[cls, 0]
        late_send(cls, 4, 1, 0, 1)

    def late2(cls):
        pair_end(cls, 2)
        late_send(cls, 3, 2, 0, 3)
        posted["l", cls, 1].wait_recv()
        ref = own_x(cls, 1, 2)
        ref[...] += r3[cls, 1]
        late_send(cls, 5, 2, 1, 3)

    def late3(cls):
        pair_end(cls, 3)
        for kind in (2, 3, 4, 5):
            posted["l", cls, kind].wait_recv()
        first = own_x(cls, 0, 3)
        first[...] += r3[cls, 4] + r3[cls, 3]
        second = own_x(cls, 1, 3)
        second[...] += r3[cls, 2] + r3[cls, 5]

    def relayout(c):
        loads["m", c].wait()

        def body(t, carry):
            k0 = pl.multiple_of(t * 64, 64)
            wbuf[:, pl.ds(k0, 64), :] = jnp.swapaxes(mbuf[c, pl.ds(k0, 64)], 0, 1)
            return carry

        lax.fori_loop(0, DEPTH // 64, body, 0)

    def product(c, cls):
        zp = lax.rem(z + CHUNKS[c], 4)

        def body(t, carry):
            j = 2 * cls + t
            for i in range(NI):
                got = lax.dot_general(wbuf[j], ubuf[i], (((0,), (0,)), ((), ())), preferred_element_type=F32)
                part[j, i, zp] = got.reshape(2, 4, 32, 256)
            return carry

        lax.fori_loop(0, 2, body, 0)

    def ladder_product():
        loads["amp"].wait()
        loads["lad"].wait()
        rounded = amp[...].reshape(256, 256).astype(jnp.bfloat16)
        row = lax.broadcasted_iota(jnp.int32, (32, 256), 0)
        lane = lax.broadcasted_iota(jnp.int32, (32, 256), 1)
        same = jnp.where(lax.rem(lane, 32) == row, 1.0, 0.0).astype(F32)

        def body(t, carry):
            s = lax.rem(t, 4)
            r0 = pl.multiple_of(t // 4 * 8, 8)
            ints = lbuf[pl.ds(r0, 8), s].reshape(256, 256)
            full = lax.dot_general(ints, rounded, (((1,), (1,)), ((), ())), preferred_element_type=F32)
            lgrp[s, pl.ds(r0, 8), :] = jnp.sum(full.reshape(8, 32, 256) * same[None], axis=1)
            return carry

        lax.fori_loop(0, 32, body, 0)
        group = lax.broadcasted_iota(jnp.int32, (256, 128), 0) // 32
        slot = lax.broadcasted_iota(jnp.int32, (256, 128), 1)
        pick = jnp.where(group == slot, 1.0, 0.0).astype(F32)
        lsum[...] = jnp.dot(
            lgrp[...].reshape(256, 256), pick, precision=lax.Precision.HIGHEST, preferred_element_type=F32
        ).reshape(4, 4, 2, 8, 128)
        for d in range(1, 4):
            peer_narrow = lax.rem(narrow + d, 4)
            send(("n", d), lsum.at[peer_narrow], lrecv_n.at[d - 1], sl.at[d - 1], ql.at[d - 1],
                 {"wide": wide, "narrow": peer_narrow})

    def ladder_z():
        for d in range(1, 4):
            posted["n", d].wait_recv()
        lsum[narrow] = lsum[narrow] + lrecv_n[0] + lrecv_n[1] + lrecv_n[2]
        for d in range(1, 4):
            send(("lz", d), lsum.at[narrow, lax.rem(z + d, 4)], lrecv_z.at[d - 1], sl.at[2 + d], ql.at[2 + d],
                 along("z", d))

    def ladder_x():
        for d in range(1, 4):
            posted["lz", d].wait_recv()
        lsum[narrow, z] = lsum[narrow, z] + lrecv_z[0] + lrecv_z[1] + lrecv_z[2]
        send("lx", lsum.at[narrow, z, 1 - xh], lrecv_x, sl.at[6], ql.at[6], along("x", 2))

    def ladder_y():
        posted["lx"].wait_recv()
        lsum[narrow, z, xh] = lsum[narrow, z, xh] + lrecv_x[...]
        for d in range(1, 4):
            send(("ly", d), lsum.at[narrow, z, xh], lrecv_y.at[d - 1], sl.at[6 + d], ql.at[6 + d], along("y", d))

    def ladder_end():
        for d in range(1, 4):
            posted["ly", d].wait_recv()
        total = lsum[narrow, z, xh] + lrecv_y[0] + lrecv_y[1] + lrecv_y[2]
        row = lax.broadcasted_iota(jnp.int32, (8, 128), 0)
        return [jnp.sum(jnp.where(row == 2 * y + e, total, 0.0), axis=0, keepdims=True) for e in range(2)]

    def fold(x):
        eight = jnp.sum(x.reshape(4, 8, 256), axis=0)
        return eight[:, :128] + eight[:, 128:]

    def tail(cls, ladder_rows, sums):
        row = lax.broadcasted_iota(jnp.int32, (32, 256), 0)
        lane = lax.broadcasted_iota(jnp.int32, (32, 256), 1)
        lane1 = lax.broadcasted_iota(jnp.int32, (1, 128), 1)
        lanes = lax.broadcasted_iota(jnp.int32, (32, 128), 1)
        rows = lax.broadcasted_iota(jnp.int32, (32, 128), 0)
        block = vir[:, pl.ds(pl.multiple_of(wide // 4 * 128, 128), 128)]
        down = jnp.sum(jnp.where(lanes == lax.rem(wide, 4) * 32 + rows, block, 0.0), axis=1, keepdims=True)
        across = vir[:, pl.ds(pl.multiple_of(narrow * 256, 256), 256)]
        for j in (2 * cls, 2 * cls + 1):
            for i in range(NI):
                ij = i * NJ + j
                placed = jnp.zeros((32, 256), F32)
                for e in range(2):
                    one = jnp.sum(jnp.where(lane1 == ij, ladder_rows[e], 0.0), axis=1, keepdims=True)
                    placed = jnp.where((row == e) & (lane == 0), one, placed)
                denominator = down + across - of_ref[i] - os_ref[j]
                a = amp[i, j]
                v = itg[i, j]
                r = v + part[j, i, z, xh, y] + placed - denominator * a
                new = a + r / denominator
                res[i, j] = r
                upd[i, j] = new
                terms = [new * v] + [his[h, i, j] * r for h in range(4)] + [r * r]
                sums = [s + fold(t) for s, t in zip(sums, terms)]
        return sums

    loads["u"].wait()
    relayout(0)
    product(0, 0)
    pl.semaphore_wait(barrier, len(greeted))
    m1(0, 0)
    m1(0, 1)
    product(0, 1)
    m1(1, 0)
    m2_up(1, 0)
    m2_down(1, 0)
    m1(0, 2)
    m1(0, 3)

    relayout(1)
    m3_up(1, 0)
    m3_down(1, 0)
    product(1, 0)
    m2_up(0, 0)
    m3_up(0, 0)
    product(1, 1)
    m1(1, 1)
    m2_up(1, 1)
    m2_down(1, 1)

    relayout(2)
    ring_end(1, 0)
    m3_up(1, 1)
    m3_down(1, 1)
    product(2, 0)
    m2_down(0, 0)
    m3_down(0, 0)
    m2_up(0, 1)
    m2_down(0, 1)
    m3_up(0, 1)
    m3_down(0, 1)
    product(2, 1)
    m1(1, 2)
    m2_up(1, 2)
    m2_down(1, 2)

    relayout(3)
    late0(1)
    m3_up(1, 2)
    m3_down(1, 2)
    product(3, 0)
    ring_end(1, 1)
    product(3, 1)
    m1(1, 3)
    m2_up(1, 3)
    m2_down(1, 3)
    ring_end(0, 0)

    def both(c):
        m2_up(0, c)
        m2_down(0, c)
        m3_up(0, c)
        m3_down(0, c)

    both(2)
    ladder_product()
    late1(1)
    late0(0)
    ring_end(0, 1)
    both(3)
    m3_up(1, 3)
    m3_down(1, 3)
    ladder_z()
    ring_end(1, 2)
    ladder_x()
    late1(0)
    ring_end(0, 2)
    late2(1)
    ladder_y()
    for name in ("itg", "his", "vir"):
        loads[name].wait()
    rows = ladder_end()
    late2(0)
    ring_end(1, 3)
    ring_end(0, 3)
    late3(1)
    sums = tail(1, rows, [jnp.zeros((8, 128), F32)] * 6)
    late3(0)
    sums = tail(0, rows, sums)

    stores = [pltpu.make_async_copy(upd, upd_hbm, lsem.at[10]), pltpu.make_async_copy(res, res_hbm, lsem.at[11])]
    for store in stores:
        store.start()

    eight = lax.broadcasted_iota(jnp.int32, (8, 128), 0)
    tile = jnp.zeros((8, 128), F32)
    for n, s in enumerate(sums):
        tile = jnp.where(eight == n, jnp.sum(s, axis=0, keepdims=True), tile)

    def everyone(buf, own, members, devices, first):
        count = len(devices) + 1
        buf[own] = tile
        for n, (device, member) in enumerate(zip(devices, members)):
            send(("s", first + n), buf.at[own], buf.at[own], ss.at[first + n], qs.at[first + n], device)
        for n, member in enumerate(members):
            pltpu.make_async_remote_copy(
                src_ref=buf.at[own], dst_ref=buf.at[member], send_sem=ss.at[first + n], recv_sem=qs.at[first + n],
                device_id=devices[n], device_id_type=MESH,
            ).wait_recv()
        total = buf[0]
        for n in range(1, count):
            total = total + buf[n]
        return total

    def chip_member(d):
        return lax.rem(xpos + 4 - d // 2, 4) * 2 + lax.rem(core + 2 - d % 2, 2)

    tile = everyone(sc_x, xpos * 2 + core, [chip_member(d) for d in range(1, 8)],
                    [at(z, y, xpos + d // 2, core + d % 2) for d in range(1, 8)], 0)
    tile = everyone(sc_y, y, [lax.rem(y + 4 - d, 4) for d in (1, 2, 3)], [along("y", d) for d in (1, 2, 3)], 7)
    tile = everyone(sc_z, z, [lax.rem(z + 4 - d, 4) for d in (1, 2, 3)], [along("z", d) for d in (1, 2, 3)], 10)

    scale = 1.0 / 8388608.0
    tile = jnp.sum(tile, axis=1, keepdims=True) * scale
    ene_ref[0] = tile[0, 0]
    for n in range(5):
        int_ref[n] = tile[n + 1, 0]
    for store in stores:
        store.wait()
    for copy in sends:
        copy.wait_send()


def shards(amplitudes, cycle_amps, cycle_ints, ladder_ints, integrals, history, vir_energy, occ_first, occ_second):
    anywhere = pl.BlockSpec(memory_space=pl.ANY)
    smem = pl.BlockSpec(memory_space=pltpu.SMEM)
    bf16 = jnp.bfloat16
    dma = pltpu.SemaphoreType.DMA
    block = jax.ShapeDtypeStruct((NI, NJ, 32, 256), F32)
    return pl.pallas_call(
        kernel,
        out_shape=(block, block, jax.ShapeDtypeStruct((1,), F32), jax.ShapeDtypeStruct((5,), F32)),
        in_specs=[anywhere] * 7 + [smem] * 2,
        out_specs=(anywhere, anywhere, smem, smem),
        scratch_shapes=[
            pltpu.VMEM((4, DEPTH, 4, 256), bf16),
            pltpu.VMEM((NI, DEPTH, 256), bf16),
            pltpu.VMEM((4, DEPTH, 256), bf16),
            pltpu.VMEM((NJ, NI, 4, 2, 4, 32, 256), F32),
            pltpu.VMEM((2, 6, 4, 2, 2, 32, 256), F32),
            pltpu.VMEM((2, 4, 2, 2, 32, 256), F32),
            pltpu.VMEM((2, 6, 2, 32, 256), F32),
            pltpu.VMEM((64, 4, 32, 256), bf16),
            pltpu.VMEM((4, 64, 256), F32),
            pltpu.VMEM((4, 4, 2, 8, 128), F32),
            pltpu.VMEM((3, 4, 2, 8, 128), F32),
            pltpu.VMEM((3, 2, 8, 128), F32),
            pltpu.VMEM((8, 128), F32),
            pltpu.VMEM((3, 8, 128), F32),
            pltpu.VMEM((NI, NJ, 32, 256), F32),
            pltpu.VMEM((NI, NJ, 32, 256), F32),
            pltpu.VMEM((4, NI, NJ, 32, 256), F32),
            pltpu.VMEM((1, 1024), F32),
            pltpu.VMEM((NI, NJ, 32, 256), F32),
            pltpu.VMEM((NI, NJ, 32, 256), F32),
            pltpu.VMEM((8, 8, 128), F32),
            pltpu.VMEM((4, 8, 128), F32),
            pltpu.VMEM((4, 8, 128), F32),
            dma((12,)),
            dma((2, 6, 4)), dma((2, 6, 4)),
            dma((2, 4)), dma((2, 4)),
            dma((2, 6)), dma((2, 6)),
            dma((10,)), dma((10,)),
            dma((13,)), dma((13,)),
        ],
        compiler_params=pltpu.CompilerParams(
            collective_id=0, has_side_effects=True, vmem_limit_bytes=58 * 2**20
        ),
        cost_estimate=pl.CostEstimate(flops=9 * 10**9, bytes_accessed=27 * 10**6, transcendentals=0),
        name="window",
    )(
        amplitudes,
        cycle_amps.reshape(NI, DEPTH, 256),
        cycle_ints.reshape(DEPTH, 4, 1024),
        ladder_ints,
        integrals,
        history,
        vir_energy.reshape(1, 1024),
        occ_first,
        occ_second,
    )


def solution(mesh):
    spread = P(None, None, "wide", "narrow")
    return jax.shard_map(
        shards,
        mesh=mesh,
        in_specs=(
            spread,
            spread,
            P(None, "wide", None, None),
            spread,
            spread,
            P(None, None, None, "wide", "narrow"),
            P(),
            P(),
            P(),
        ),
        out_specs=(spread, spread, P(), P()),
        check_vma=False,
    )
```

```python
import jax
import jax.numpy as jnp
from jax import lax
from jax.experimental import pallas as pl
from jax.experimental.pallas import tpu as pltpu
from jax.sharding import PartitionSpec as P

NI = 2
NJ = 4
DEPTH = 2048
MESH = pl.DeviceIdType.MESH
CHUNKS = (2, 1, 3, 0)
F32 = jnp.float32


def kernel(
    amp_hbm, u_hbm, m_hbm, lad_hbm, itg_hbm, his_hbm, vir_hbm, of_hbm, os_hbm,
    upd, res, ene_ref, int_ref,
    mbuf, ubuf, wbuf, part, r0, r1, rx, rf, r3,
    lbuf, lgrp, lsum, lrecv_a, lplane, lrecv_b,
    amp, itg, his, vir, of_ref, os_ref, sums_a, sums_b,
    lsem, s0, q0, s1, q1, sx, qx, s3, q3, sl, ql, ss, qs,
):
    wide = lax.axis_index("wide")
    narrow = lax.axis_index("narrow")
    z = wide // 8
    xh = lax.rem(wide // 4, 2)
    y = lax.rem(wide, 4)
    xl = narrow // 2
    core = lax.rem(narrow, 2)
    xpos = xh * 2 + xl

    def at(z_, y_, x_, core_):
        return {
            "wide": lax.rem(z_, 4) * 8 + lax.rem(x_, 4) // 2 * 4 + lax.rem(y_, 4),
            "narrow": lax.rem(x_, 2) * 2 + lax.rem(core_, 2),
        }

    def along(axis, delta):
        if axis == "z":
            return at(z + delta, y, xpos, core)
        if axis == "y":
            return at(z, y + delta, xpos, core)
        return at(z, y, xpos + delta, core)

    barrier = pltpu.get_barrier_semaphore()
    plane = [at(z + d // 4, y + d % 4, xpos, core) for d in range(1, 16)]
    row_of_chips = [at(z, y, xpos + d // 2, core + d % 2) for d in range(1, 8)]
    for device in plane + row_of_chips:
        pl.semaphore_signal(barrier, inc=1, device_id=device, device_id_type=MESH)

    loads = {}

    def load(name, src, dst, n):
        loads[name] = pltpu.make_async_copy(src, dst, lsem.at[n])
        loads[name].start()

    def columns(c, x0, width):
        zc = lax.rem(z + CHUNKS[c], 4)
        return pl.ds(pl.multiple_of(zc * 256 + x0, 128), width)

    for q in range(4):
        rows_q = pl.ds(q * (DEPTH // 4), DEPTH // 4)
        load(("q", q), m_hbm.at[rows_q, :, columns(0, 0, 256)], mbuf.at[0, rows_q], 12 + q)
    load("u", u_hbm, ubuf, 0)

    def load_rest():
        for c in (3, 1, 2):
            load(("m", c), m_hbm.at[:, :, columns(c, 0, 256)], mbuf.at[c], 1 + c)
        load("amp", amp_hbm, amp, 5)
        load("lad", lad_hbm, lbuf, 6)
        load("itg", itg_hbm, itg, 7)
        load("his", his_hbm, his, 8)
        load("vir", vir_hbm, vir, 9)
        load("of", of_hbm, of_ref, 1)
        load("os", os_hbm, os_ref, 16)

    sends = []
    posted = {}

    def send(key, src, dst, ssem, rsem, device):
        copy = pltpu.make_async_remote_copy(
            src_ref=src, dst_ref=dst, send_sem=ssem, recv_sem=rsem, device_id=device, device_id_type=MESH
        )
        copy.start()
        sends.append(copy)
        posted[key] = copy

    ring_axis = ("z", "y")
    ring_pos = (z, y)
    chunk_pos = (y, z)

    def places(cls, ring_offset, c):
        ring = lax.rem(ring_pos[cls] + ring_offset, 4)
        chunk = lax.rem(chunk_pos[cls] + CHUNKS[c], 4)
        return (ring, chunk) if cls == 0 else (chunk, ring)

    def x_first(cls, c):
        return cls == 1 and c == 3

    def whole(cls, i, ring_offset, c):
        zp, yp = places(cls, ring_offset, c)
        return part.at[pl.ds(2 * cls, 2), i, zp, xh if x_first(cls, c) else slice(None), yp]

    def landing(cls, kind, c):
        return r1.at[cls, kind, c, :, 0] if x_first(cls, c) else r1.at[cls, kind, c]

    def first_pair():
        send("f", part.at[pl.ds(2, 2), :, z, 1 - xh], rf, sx.at[1, 3], qx.at[1, 3], along("x", 2))

    def first_pair_end():
        posted["f"].wait_recv()
        part[pl.ds(2, 2), :, z, xh] += rf[...]

    def own_x(cls, i, c):
        zp, yp = places(cls, 0, c)
        return part.at[pl.ds(2 * cls, 2), i, zp, xh, yp]

    def ring_send(cls, kind, c, i, ring_offset, step):
        send(("r", cls, kind, c), whole(cls, i, ring_offset, c), landing(cls, kind, c),
             s1.at[cls, kind, c], q1.at[cls, kind, c], along(ring_axis[cls], step))

    def m1(cls, c):
        ring_send(cls, 0, c, 0, 2, 1)
        ring_send(cls, 1, c, 1, 2, 3)

    def m1_one(j):
        zp = lax.rem(z + 2, 4)
        for i, step in ((0, 1), (1, 3)):
            send(("h", i, j), part.at[j, i, zp], r0.at[i, j], s0.at[i, j], q0.at[i, j], along("z", step))

    def early(cls, i, c, zp, yp):
        if cls == 1:
            posted["r", cls, i, c].wait_recv()
            ref = whole(cls, i, 1 + 2 * i, c)
            ref[...] += landing(cls, i, c)[...]
            return
        for j in range(2):
            if c == 0:
                posted["h", i, j].wait_recv()
            part[j, i, zp, :, yp] += r0[i, j, :, yp]

    def m2_up(cls, c):
        ring_send(cls, 2, c, 1, 1, 1)

    def m2_down(cls, c):
        ring_send(cls, 3, c, 0, 3, 3)

    def m3_up(cls, c):
        early(cls, 0, c, *places(cls, 1, c))
        ring_send(cls, 4, c, 0, 1, 1)

    def m3_down(cls, c):
        early(cls, 1, c, *places(cls, 3, c))
        ring_send(cls, 5, c, 1, 3, 3)

    def ring_end(cls, c):
        for kind in (2, 3, 4, 5):
            posted["r", cls, kind, c].wait_recv()
        first = whole(cls, 0, 0, c)
        first[...] += landing(cls, 4, c)[...] + landing(cls, 3, c)[...]
        second = whole(cls, 1, 0, c)
        second[...] += landing(cls, 2, c)[...] + landing(cls, 5, c)[...]
        if x_first(cls, c):
            return
        zp, yp = places(cls, 0, c)
        send(("x", cls, c), part.at[pl.ds(2 * cls, 2), :, zp, 1 - xh, yp], rx.at[cls, c],
             sx.at[cls, c], qx.at[cls, c], along("x", 2))

    def pair_end(cls, c):
        if x_first(cls, c):
            return
        posted["x", cls, c].wait_recv()
        zp, yp = places(cls, 0, c)
        ref = part.at[pl.ds(2 * cls, 2), :, zp, xh, yp]
        ref[...] += rx[cls, c]

    def late_send(cls, kind, c, i, step):
        send(("l", cls, kind), own_x(cls, i, c), r3.at[cls, kind], s3.at[cls, kind], q3.at[cls, kind],
             along(ring_axis[1 - cls], step))

    def late0(cls):
        pair_end(cls, 0)
        late_send(cls, 0, 0, 0, 1)
        late_send(cls, 1, 0, 1, 3)

    def late1(cls):
        pair_end(cls, 1)
        late_send(cls, 2, 1, 1, 1)
        posted["l", cls, 0].wait_recv()
        ref = own_x(cls, 0, 1)
        ref[...] += r3[cls, 0]
        late_send(cls, 4, 1, 0, 1)

    def late2(cls):
        pair_end(cls, 2)
        late_send(cls, 3, 2, 0, 3)
        posted["l", cls, 1].wait_recv()
        ref = own_x(cls, 1, 2)
        ref[...] += r3[cls, 1]
        late_send(cls, 5, 2, 1, 3)

    def late3(cls):
        pair_end(cls, 3)
        for kind in (2, 3, 4, 5):
            posted["l", cls, kind].wait_recv()
        first = own_x(cls, 0, 3)
        first[...] += r3[cls, 4] + r3[cls, 3]
        second = own_x(cls, 1, 3)
        second[...] += r3[cls, 2] + r3[cls, 5]

    def relayout(c, b):
        def body(t, carry):
            k0 = pl.multiple_of(t * 64, 64)
            wbuf[b, :, pl.ds(k0, 64), :] = jnp.swapaxes(mbuf[c, pl.ds(k0, 64)], 0, 1)
            return carry

        steps = DEPTH // 64
        if c:
            loads["m", c].wait()
            lax.fori_loop(0, steps, body, 0)
            return
        for q in range(4):
            loads["q", q].wait()
            lax.fori_loop(q * steps // 4, (q + 1) * steps // 4, body, 0)

    def product(c, b, first, count=2):
        zp = lax.rem(z + CHUNKS[c], 4)

        def body(j, carry):
            for i in range(NI):
                got = lax.dot_general(wbuf[b, j], ubuf[i], (((0,), (0,)), ((), ())), preferred_element_type=F32)
                part[j, i, zp] = got.reshape(2, 4, 32, 256)
            return carry

        lax.fori_loop(first, first + count, body, 0)

    def ladder_part(s):
        if s == 0:
            loads["amp"].wait()
            loads["lad"].wait()
        rounded = amp[...].reshape(256, 256).astype(jnp.bfloat16)
        row = lax.broadcasted_iota(jnp.int32, (32, 256), 0)
        lane = lax.broadcasted_iota(jnp.int32, (32, 256), 1)
        same = jnp.where(lax.rem(lane, 32) == row, 1.0, 0.0).astype(F32)

        def body(t, carry):
            r0_ = pl.multiple_of(t * 16, 16)
            ints = lbuf[pl.ds(r0_, 16), s].reshape(512, 256)
            full = lax.dot_general(ints, rounded, (((1,), (1,)), ((), ())), preferred_element_type=F32)
            lgrp[s, pl.ds(r0_, 16), :] = jnp.sum(full.reshape(16, 32, 256) * same[None], axis=1)
            return carry

        lax.fori_loop(0, 4, body, 0)

    def ladder_lanes():
        group = lax.broadcasted_iota(jnp.int32, (256, 128), 0) // 32
        slot = lax.broadcasted_iota(jnp.int32, (256, 128), 1)
        pick = jnp.where(group == slot, 1.0, 0.0).astype(F32)
        lsum[...] = jnp.dot(
            lgrp[...].reshape(256, 256), pick, precision=lax.Precision.HIGHEST, preferred_element_type=F32
        ).reshape(4, 4, 2, 8, 128)
        for d in range(1, 8):
            xd = lax.rem(xpos + d // 2, 4)
            cd = lax.rem(core + d % 2, 2)
            pltpu.make_async_remote_copy(
                src_ref=lsum.at[lax.rem(xd, 2) * 2 + cd, :, xd // 2], dst_ref=lrecv_a.at[d - 1],
                send_sem=sl.at[0], recv_sem=ql.at[0], device_id=at(z, y, xd, cd), device_id_type=MESH,
            ).start()

    def arrivals(ref, n):
        return pltpu.make_async_remote_copy(
            src_ref=ref, dst_ref=ref, send_sem=sl.at[n], recv_sem=ql.at[n], device_id=plane[0], device_id_type=MESH
        )

    def ladder_plane():
        arrivals(lrecv_a, 0).wait_recv()
        lplane[...] = lsum[narrow, :, xh] + jnp.sum(lrecv_a[...], axis=0)
        for d in range(1, 16):
            pltpu.make_async_remote_copy(
                src_ref=lplane.at[lax.rem(z + d // 4, 4)], dst_ref=lrecv_b.at[d - 1],
                send_sem=sl.at[1], recv_sem=ql.at[1], device_id=plane[d - 1], device_id_type=MESH,
            ).start()

    def ladder_end():
        arrivals(lrecv_b, 1).wait_recv()
        total = lplane[z] + jnp.sum(lrecv_b[...], axis=0)
        row = lax.broadcasted_iota(jnp.int32, (8, 128), 0)
        return [jnp.sum(jnp.where(row == 2 * y + e, total, 0.0), axis=0, keepdims=True) for e in range(2)]

    def fold(x):
        eight = jnp.sum(x.reshape(4, 8, 256), axis=0)
        return eight[:, :128] + eight[:, 128:]

    def tail(cls, ladder_rows, sums):
        row = lax.broadcasted_iota(jnp.int32, (32, 256), 0)
        lane = lax.broadcasted_iota(jnp.int32, (32, 256), 1)
        lane1 = lax.broadcasted_iota(jnp.int32, (1, 128), 1)
        lanes = lax.broadcasted_iota(jnp.int32, (32, 128), 1)
        rows = lax.broadcasted_iota(jnp.int32, (32, 128), 0)
        block = vir[:, pl.ds(pl.multiple_of(wide // 4 * 128, 128), 128)]
        down = jnp.sum(jnp.where(lanes == lax.rem(wide, 4) * 32 + rows, block, 0.0), axis=1, keepdims=True)
        across = vir[:, pl.ds(pl.multiple_of(narrow * 256, 256), 256)]
        for j in (2 * cls, 2 * cls + 1):
            for i in range(NI):
                ij = i * NJ + j
                placed = jnp.zeros((32, 256), F32)
                for e in range(2):
                    one = jnp.sum(jnp.where(lane1 == ij, ladder_rows[e], 0.0), axis=1, keepdims=True)
                    placed = jnp.where((row == e) & (lane == 0), one, placed)
                denominator = down + across - of_ref[:, i : i + 1] - os_ref[:, j : j + 1]
                a = amp[i, j]
                v = itg[i, j]
                r = v + part[j, i, z, xh, y] + placed - denominator * a
                new = a + r / denominator
                res[i, j] = r
                upd[i, j] = new
                terms = [new * v] + [his[h, i, j] * r for h in range(4)] + [r * r]
                sums = [s + fold(t) for s, t in zip(sums, terms)]
        return sums

    def paced(*keys):
        for key in keys:
            sends.remove(posted[key])
            posted[key].wait_send()

    def paced_ring(cls, c, *kinds):
        paced(*[("r", cls, kind, c) for kind in kinds])

    relayout(0, 0)
    loads["u"].wait()
    load_rest()
    product(0, 0, 0, 1)
    pl.semaphore_wait(barrier, len(plane + row_of_chips))
    m1_one(0)
    product(0, 0, 1, 1)
    m1_one(1)
    product(0, 0, 2)
    m1(1, 0)
    relayout(3, 0)
    product(3, 0, 2)
    first_pair()
    m2_up(1, 0)
    m2_down(1, 0)
    relayout(1, 1)
    product(1, 1, 0)
    m3_up(1, 0)
    m3_down(1, 0)
    product(1, 1, 2)
    m1(1, 1)
    m2_up(0, 0)
    relayout(2, 1)
    product(2, 1, 0)
    m2_down(0, 0)
    m2_up(1, 1)
    m2_down(1, 1)
    product(2, 1, 2)
    ring_end(1, 0)
    m3_up(0, 0)
    m3_down(0, 0)
    product(3, 0, 0)
    m3_up(1, 1)
    m3_down(1, 1)
    m2_up(0, 1)
    m2_down(0, 1)
    ladder_part(0)
    m3_up(0, 1)
    m3_down(0, 1)
    m1(1, 2)
    ladder_part(1)
    ladder_part(2)
    m2_up(1, 2)
    m2_down(1, 2)
    ladder_part(3)
    ladder_lanes()
    ring_end(0, 0)
    m2_up(0, 2)
    m2_down(0, 2)
    ring_end(1, 1)
    first_pair_end()
    m1(1, 3)
    late0(1)
    m3_up(1, 2)
    m3_down(1, 2)
    m3_up(0, 2)
    m3_down(0, 2)
    ring_end(0, 1)
    m2_up(0, 3)
    m2_down(0, 3)
    late0(0)
    m2_up(1, 3)
    m2_down(1, 3)
    late1(1)
    ring_end(1, 2)
    m3_up(1, 3)
    m3_down(1, 3)
    m3_up(0, 3)
    m3_down(0, 3)
    late1(0)
    ladder_plane()
    ring_end(0, 2)
    late2(1)
    late2(0)
    for name in ("itg", "his", "vir", "of", "os"):
        loads[name].wait()
    ring_end(0, 3)
    ring_end(1, 3)
    rows = ladder_end()
    late3(1)
    sums = tail(1, rows, [jnp.zeros((8, 128), F32)] * 6)
    late3(0)
    sums = tail(0, rows, sums)

    lane = lax.broadcasted_iota(jnp.int32, (1, 128), 1)
    mine = jnp.zeros((1, 128), F32)
    for n, s in enumerate(sums):
        one = jnp.sum(jnp.sum(s, axis=0, keepdims=True), axis=1, keepdims=True)
        mine = jnp.where(lane == n, one, mine)

    def everyone(buf, own, row, devices, n):
        count = len(devices)
        buf[own] = row
        for device in devices:
            pltpu.make_async_remote_copy(
                src_ref=buf.at[own], dst_ref=buf.at[own], send_sem=ss.at[n], recv_sem=qs.at[n],
                device_id=device, device_id_type=MESH,
            ).start()
        arrived = pltpu.make_async_remote_copy(
            src_ref=buf.at[pl.ds(0, count)], dst_ref=buf.at[pl.ds(0, count)], send_sem=ss.at[n], recv_sem=qs.at[n],
            device_id=devices[0], device_id_type=MESH,
        )
        arrived.wait_recv()
        return jnp.sum(buf[...], axis=0), arrived

    def totals():
        row, first = everyone(sums_a, z * 4 + y, mine, plane, 0)
        row, second = everyone(sums_b, xpos * 2 + core, row, row_of_chips, 1)
        row = row * (1.0 / 8388608.0)
        ene_ref[0] = row[0, 0]
        for n in range(5):
            int_ref[n] = row[0, n + 1]
        first.wait_send()
        second.wait_send()

    totals()
    arrivals(lrecv_a, 0).wait_send()
    arrivals(lrecv_b, 1).wait_send()
    for copy in sends:
        copy.wait_send()


def shards(amplitudes, cycle_amps, cycle_ints, ladder_ints, integrals, history, vir_energy, occ_first, occ_second):
    smem = pl.BlockSpec(memory_space=pltpu.SMEM)
    bf16 = jnp.bfloat16
    dma = pltpu.SemaphoreType.DMA
    block = pltpu.VMEM((NI, NJ, 32, 256), F32)
    vmem = pl.BlockSpec(memory_space=pltpu.VMEM)
    return pl.pallas_call(
        kernel,
        out_shape=(block, block, jax.ShapeDtypeStruct((1,), F32), jax.ShapeDtypeStruct((5,), F32)),
        in_specs=[pl.BlockSpec(memory_space=pltpu.HBM)] * 9,
        out_specs=(vmem, vmem, smem, smem),
        scratch_shapes=[
            pltpu.VMEM((4, DEPTH, 4, 256), bf16),
            pltpu.VMEM((NI, DEPTH, 256), bf16),
            pltpu.VMEM((2, 4, DEPTH, 256), bf16),
            pltpu.VMEM((NJ, NI, 4, 2, 4, 32, 256), F32),
            pltpu.VMEM((2, 2, 2, 4, 32, 256), F32),
            pltpu.VMEM((2, 6, 4, 2, 2, 32, 256), F32),
            pltpu.VMEM((2, 4, 2, 2, 32, 256), F32),
            pltpu.VMEM((2, 2, 4, 32, 256), F32),
            pltpu.VMEM((2, 6, 2, 32, 256), F32),
            pltpu.VMEM((64, 4, 32, 256), bf16),
            pltpu.VMEM((4, 64, 256), F32),
            pltpu.VMEM((4, 4, 2, 8, 128), F32),
            pltpu.VMEM((7, 4, 8, 128), F32),
            pltpu.VMEM((4, 8, 128), F32),
            pltpu.VMEM((15, 8, 128), F32),
            pltpu.VMEM((NI, NJ, 32, 256), F32),
            pltpu.VMEM((NI, NJ, 32, 256), F32),
            pltpu.VMEM((4, NI, NJ, 32, 256), F32),
            pltpu.VMEM((1, 1024), F32),
            pltpu.VMEM((1, NI), F32),
            pltpu.VMEM((1, NJ), F32),
            pltpu.VMEM((16, 1, 128), F32),
            pltpu.VMEM((8, 1, 128), F32),
            dma((17,)),
            dma((2, 2)), dma((2, 2)),
            dma((2, 6, 4)), dma((2, 6, 4)),
            dma((2, 4)), dma((2, 4)),
            dma((2, 6)), dma((2, 6)),
            dma((2,)), dma((2,)),
            dma((2,)), dma((2,)),
        ],
        compiler_params=pltpu.CompilerParams(
            collective_id=0, has_side_effects=True, vmem_limit_bytes=52 * 2**20
        ),
        cost_estimate=pl.CostEstimate(flops=9 * 10**9, bytes_accessed=27 * 10**6, transcendentals=0),
        name="window",
    )(*(pltpu.with_memory_space_constraint(x, pltpu.HBM) for x in (
        amplitudes,
        cycle_amps.reshape(NI, DEPTH, 256),
        cycle_ints.reshape(DEPTH, 4, 1024),
        ladder_ints,
        integrals,
        history,
        vir_energy.reshape(1, 1024),
        occ_first.reshape(1, NI),
        occ_second.reshape(1, NJ),
    )))


def solution(mesh):
    spread = P(None, None, "wide", "narrow")
    return jax.shard_map(
        shards,
        mesh=mesh,
        in_specs=(
            spread,
            spread,
            P(None, "wide", None, None),
            spread,
            spread,
            P(None, None, None, "wide", "narrow"),
            P(),
            P(),
            P(),
        ),
        out_specs=(spread, spread, P(), P()),
        check_vma=False,
    )
```

```python
import jax
import jax.numpy as jnp
from jax import lax
from jax.experimental import pallas as pl
from jax.experimental.pallas import tpu as pltpu
from jax.sharding import PartitionSpec as P

NI = 2
NJ = 4
DEPTH = 2048
MESH = pl.DeviceIdType.MESH
CHUNKS = (2, 1, 3, 0)
F32 = jnp.float32


def kernel(
    amp_hbm, u_hbm, m_hbm, lad_hbm, itg_hbm, his_hbm, vir_hbm, of_hbm, os_hbm,
    both_ref, tot_ref,
    mbuf, ubuf, wbuf, part, r0, r1, rx, rf, r3,
    lbuf, lgrp, lsum, lrecv_a, lplane, lrecv_b,
    amp, itg, his, vir, of_ref, os_ref, sums_a, sums_b,
    lsem, sent, q0, q1, qe, qx, q3, qf, sl, ql, ss, qs,
):
    wide = lax.axis_index("wide")
    narrow = lax.axis_index("narrow")
    z = wide // 8
    xh = lax.rem(wide // 4, 2)
    y = lax.rem(wide, 4)
    xl = narrow // 2
    core = lax.rem(narrow, 2)
    xpos = xh * 2 + xl

    def at(z_, y_, x_, core_):
        return {
            "wide": lax.rem(z_, 4) * 8 + lax.rem(x_, 4) // 2 * 4 + lax.rem(y_, 4),
            "narrow": lax.rem(x_, 2) * 2 + lax.rem(core_, 2),
        }

    def along(axis, delta):
        if axis == "z":
            return at(z + delta, y, xpos, core)
        if axis == "y":
            return at(z, y + delta, xpos, core)
        return at(z, y, xpos + delta, core)

    barrier = pltpu.get_barrier_semaphore()
    plane = [at(z + d // 4, y + d % 4, xpos, core) for d in range(1, 16)]
    row_of_chips = [at(z, y, xpos + d // 2, core + d % 2) for d in range(1, 8)]
    for device in plane + row_of_chips:
        pl.semaphore_signal(barrier, inc=1, device_id=device, device_id_type=MESH)

    loads = {}

    def load(name, src, dst, n):
        loads[name] = pltpu.make_async_copy(src, dst, lsem.at[n])
        loads[name].start()

    def columns(c, x0, width):
        zc = lax.rem(z + CHUNKS[c], 4)
        return pl.ds(pl.multiple_of(zc * 256 + x0, 128), width)

    for q in range(4):
        rows_q = pl.ds(q * (DEPTH // 4), DEPTH // 4)
        load(("q", q), m_hbm.at[rows_q, :, columns(0, 0, 256)], mbuf.at[0, rows_q], 12 + q)
    load("u", u_hbm, ubuf, 0)

    def load_rest():
        for c in (3, 1, 2):
            load(("m", c), m_hbm.at[:, :, columns(c, 0, 256)], mbuf.at[c], 1 + c)
        load("amp", amp_hbm, amp, 5)
        load("lad", lad_hbm, lbuf, 6)
        load("itg", itg_hbm, itg, 7)
        load("his", his_hbm, his, 8)
        load("vir", vir_hbm, vir, 9)
        load("of", of_hbm, of_ref, 1)
        load("os", os_hbm, os_ref, 16)

    def send(src, dst, group, rsem, device):
        pltpu.make_async_remote_copy(
            src_ref=src, dst_ref=dst, send_sem=sent.at[group], recv_sem=rsem, device_id=device, device_id_type=MESH
        ).start()

    def all_sent():
        groups = (r0, r1.at[0, pl.ds(2, 4)], r1.at[1, :, pl.ds(0, 3)], r1.at[1, :, 3, :, 0],
                  rx.at[0], rx.at[1, pl.ds(0, 3)], rf, r3.at[0], r3.at[1])
        for group, ref in enumerate(groups):
            pltpu.make_async_remote_copy(
                src_ref=ref, dst_ref=ref, send_sem=sent.at[group], recv_sem=q0.at[0], device_id=plane[0],
                device_id_type=MESH,
            ).wait_send()

    ring_axis = ("z", "y")
    ring_pos = (z, y)
    chunk_pos = (y, z)

    def places(cls, ring_offset, c):
        ring = lax.rem(ring_pos[cls] + ring_offset, 4)
        chunk = lax.rem(chunk_pos[cls] + CHUNKS[min(c, 3)], 4)
        return (ring, chunk) if cls == 0 else (chunk, ring)

    def js(cls, c):
        return pl.ds(c - 3, 1) if cls == 0 and c >= 3 else pl.ds(2 * cls, 2)

    def x_first(cls, c):
        return cls == 1 and c == 3

    def whole(cls, i, ring_offset, c):
        zp, yp = places(cls, ring_offset, c)
        return part.at[js(cls, c), i, zp, xh if x_first(cls, c) else slice(None), yp]

    def landing(cls, kind, c):
        if x_first(cls, c):
            return r1.at[cls, kind, c, :, 0]
        if cls == 0 and c >= 3:
            return r1.at[cls, kind, 3, js(cls, c)]
        return r1.at[cls, kind, c]

    def wait_bytes(ref, sem):
        pltpu.make_async_remote_copy(
            src_ref=ref, dst_ref=ref, send_sem=sent.at[0], recv_sem=sem, device_id=plane[0], device_id_type=MESH
        ).wait_recv()

    def first_pair():
        send(part.at[pl.ds(2, 2), :, z, 1 - xh], rf, 6, qf.at[0], along("x", 2))

    def first_pair_end():
        wait_bytes(rf, qf.at[0])
        part[pl.ds(2, 2), :, z, xh] += rf[...]

    def ring_send(cls, kind, c, i, ring_offset, step):
        send(whole(cls, i, ring_offset, c), landing(cls, kind, c), 2 + x_first(cls, c) if cls else 1,
             q1.at[kind, c] if kind < 2 else qe.at[cls, c], along(ring_axis[cls], step))

    def m1(cls, c):
        ring_send(cls, 0, c, 0, 2, 1)
        ring_send(cls, 1, c, 1, 2, 3)

    def m1_one(j):
        zp = lax.rem(z + 2, 4)
        for i, step in ((0, 1), (1, 3)):
            send(part.at[j, i, zp], r0.at[i, j], 0, q0.at[i], along("z", step))

    def early(cls, i, c):
        ref = whole(cls, i, 1 + 2 * i, c)
        if cls == 1:
            wait_bytes(landing(cls, i, c), q1.at[i, c])
            ref[...] += landing(cls, i, c)[...]
            return
        if c == 0:
            wait_bytes(r0.at[i], q0.at[i])
        ref[...] += r0[i, js(cls, c), :, places(cls, 0, c)[1]]

    def m2_up(cls, c):
        ring_send(cls, 2, c, 1, 1, 1)

    def m2_down(cls, c):
        ring_send(cls, 3, c, 0, 3, 3)

    def m3_up(cls, c):
        early(cls, 0, c)
        ring_send(cls, 4, c, 0, 1, 1)

    def m3_down(cls, c):
        early(cls, 1, c)
        ring_send(cls, 5, c, 1, 3, 3)

    def ring_end(cls, c):
        if x_first(cls, c):
            wait_bytes(r1.at[cls, pl.ds(2, 4), c, :, 0], qe.at[cls, c])
        elif cls == 0 and c >= 3:
            wait_bytes(r1.at[cls, pl.ds(2, 4), 3, js(cls, c)], qe.at[cls, c])
        else:
            wait_bytes(r1.at[cls, pl.ds(2, 4), c], qe.at[cls, c])
        first = whole(cls, 0, 0, c)
        first[...] += landing(cls, 4, c)[...] + landing(cls, 3, c)[...]
        second = whole(cls, 1, 0, c)
        second[...] += landing(cls, 2, c)[...] + landing(cls, 5, c)[...]
        if x_first(cls, c):
            return
        zp, yp = places(cls, 0, c)
        send(part.at[js(cls, c), :, zp, 1 - xh, yp], paired(cls, c), 4 + cls, qx.at[cls, c], along("x", 2))

    def paired(cls, c):
        return rx.at[cls, 3, js(cls, c)] if cls == 0 and c >= 3 else rx.at[cls, c]

    def pair_end(cls, c):
        if x_first(cls, c):
            return
        wait_bytes(paired(cls, c), qx.at[cls, c])
        zp, yp = places(cls, 0, c)
        ref = part.at[js(cls, c), :, zp, xh, yp]
        ref[...] += paired(cls, c)[...]

    def own_x(cls, i, c):
        zp, yp = places(cls, 0, c)
        return part.at[pl.ds(2 * cls, 2), i, zp, xh, yp]

    def late_send(cls, kind, c, i, step):
        send(own_x(cls, i, c), r3.at[cls, kind], 7 + cls, q3.at[cls, min(kind, 2)], along(ring_axis[1 - cls], step))

    def late0(cls):
        pair_end(cls, 0)
        late_send(cls, 0, 0, 0, 1)
        late_send(cls, 1, 0, 1, 3)

    def late1(cls):
        pair_end(cls, 1)
        late_send(cls, 2, 1, 1, 1)
        wait_bytes(r3.at[cls, 0], q3.at[cls, 0])
        ref = own_x(cls, 0, 1)
        ref[...] += r3[cls, 0]
        late_send(cls, 4, 1, 0, 1)

    def late2(cls):
        pair_end(cls, 2)
        late_send(cls, 3, 2, 0, 3)
        wait_bytes(r3.at[cls, 1], q3.at[cls, 1])
        ref = own_x(cls, 1, 2)
        ref[...] += r3[cls, 1]
        late_send(cls, 5, 2, 1, 3)

    def late3(cls):
        wait_bytes(r3.at[cls, pl.ds(2, 4)], q3.at[cls, 2])
        pair_end(cls, 3)
        if cls == 0:
            pair_end(cls, 4)
        first = own_x(cls, 0, 3)
        first[...] += r3[cls, 4] + r3[cls, 3]
        second = own_x(cls, 1, 3)
        second[...] += r3[cls, 2] + r3[cls, 5]

    def relayout(c, b):
        def body(t, carry):
            k0 = pl.multiple_of(t * 64, 64)
            wbuf[b, :, pl.ds(k0, 64), :] = jnp.swapaxes(mbuf[c, pl.ds(k0, 64)], 0, 1)
            return carry

        steps = DEPTH // 64
        if c:
            loads["m", c].wait()
            lax.fori_loop(0, steps, body, 0)
            return
        for q in range(4):
            loads["q", q].wait()
            lax.fori_loop(q * steps // 4, (q + 1) * steps // 4, body, 0)

    def product(c, b, first, count=2):
        zp = lax.rem(z + CHUNKS[c], 4)

        def body(j, carry):
            for i in range(NI):
                got = lax.dot_general(wbuf[b, j], ubuf[i], (((0,), (0,)), ((), ())), preferred_element_type=F32)
                part[j, i, zp] = got.reshape(2, 4, 32, 256)
            return carry

        lax.fori_loop(first, first + count, body, 0)

    def ladder_part(s):
        if s == 0:
            loads["amp"].wait()
            loads["lad"].wait()
        rounded = amp[...].reshape(256, 256).astype(jnp.bfloat16)
        row = lax.broadcasted_iota(jnp.int32, (32, 256), 0)
        lane = lax.broadcasted_iota(jnp.int32, (32, 256), 1)
        same = jnp.where(lax.rem(lane, 32) == row, 1.0, 0.0).astype(F32)

        def body(t, carry):
            r0_ = pl.multiple_of(t * 16, 16)
            ints = lbuf[pl.ds(r0_, 16), s].reshape(512, 256)
            full = lax.dot_general(ints, rounded, (((1,), (1,)), ((), ())), preferred_element_type=F32)
            lgrp[s, pl.ds(r0_, 16), :] = jnp.sum(full.reshape(16, 32, 256) * same[None], axis=1)
            return carry

        lax.fori_loop(0, 4, body, 0)

    def ladder_lanes():
        group = lax.broadcasted_iota(jnp.int32, (256, 128), 0) // 32
        slot = lax.broadcasted_iota(jnp.int32, (256, 128), 1)
        pick = jnp.where(group == slot, 1.0, 0.0).astype(F32)
        lsum[...] = jnp.dot(
            lgrp[...].reshape(256, 256), pick, precision=lax.Precision.HIGHEST, preferred_element_type=F32
        ).reshape(4, 4, 2, 8, 128)
        for d in range(1, 8):
            xd = lax.rem(xpos + d // 2, 4)
            cd = lax.rem(core + d % 2, 2)
            pltpu.make_async_remote_copy(
                src_ref=lsum.at[lax.rem(xd, 2) * 2 + cd, :, xd // 2], dst_ref=lrecv_a.at[d - 1],
                send_sem=sl.at[0], recv_sem=ql.at[0], device_id=at(z, y, xd, cd), device_id_type=MESH,
            ).start()

    def arrivals(ref, n):
        return pltpu.make_async_remote_copy(
            src_ref=ref, dst_ref=ref, send_sem=sl.at[n], recv_sem=ql.at[n], device_id=plane[0], device_id_type=MESH
        )

    def ladder_plane():
        arrivals(lrecv_a, 0).wait_recv()
        lplane[...] = lsum[narrow, :, xh] + jnp.sum(lrecv_a[...], axis=0)
        for d in range(1, 16):
            pltpu.make_async_remote_copy(
                src_ref=lplane.at[lax.rem(z + d // 4, 4)], dst_ref=lrecv_b.at[d - 1],
                send_sem=sl.at[1], recv_sem=ql.at[1], device_id=plane[d - 1], device_id_type=MESH,
            ).start()

    def ladder_end():
        arrivals(lrecv_b, 1).wait_recv()
        total = lplane[z] + jnp.sum(lrecv_b[...], axis=0)
        row = lax.broadcasted_iota(jnp.int32, (8, 128), 0)
        return [jnp.sum(jnp.where(row == 2 * y + e, total, 0.0), axis=0, keepdims=True) for e in range(2)]

    def fold(x):
        eight = jnp.sum(x.reshape(4, 8, 256), axis=0)
        return eight[:, :128] + eight[:, 128:]

    def tail(cls, ladder_rows, sums):
        row = lax.broadcasted_iota(jnp.int32, (32, 256), 0)
        lane = lax.broadcasted_iota(jnp.int32, (32, 256), 1)
        lane1 = lax.broadcasted_iota(jnp.int32, (1, 128), 1)
        lanes = lax.broadcasted_iota(jnp.int32, (32, 128), 1)
        rows = lax.broadcasted_iota(jnp.int32, (32, 128), 0)
        block = vir[:, pl.ds(pl.multiple_of(wide // 4 * 128, 128), 128)]
        down = jnp.sum(jnp.where(lanes == lax.rem(wide, 4) * 32 + rows, block, 0.0), axis=1, keepdims=True)
        across = vir[:, pl.ds(pl.multiple_of(narrow * 256, 256), 256)]
        for j in (2 * cls, 2 * cls + 1):
            for i in range(NI):
                ij = i * NJ + j
                placed = jnp.zeros((32, 256), F32)
                for e in range(2):
                    one = jnp.sum(jnp.where(lane1 == ij, ladder_rows[e], 0.0), axis=1, keepdims=True)
                    placed = jnp.where((row == e) & (lane == 0), one, placed)
                denominator = down + across - of_ref[:, i : i + 1] - os_ref[:, j : j + 1]
                a = amp[i, j]
                v = itg[i, j]
                r = v + part[j, i, z, xh, y] + placed - denominator * a
                new = a + r / denominator
                both_ref[1, i, j] = r
                both_ref[0, i, j] = new
                terms = [new * v] + [his[h, i, j] * r for h in range(4)] + [r * r]
                sums = [s + fold(t) for s, t in zip(sums, terms)]
        return sums

    relayout(0, 0)
    loads["u"].wait()
    load_rest()
    product(0, 0, 0, 1)
    pl.semaphore_wait(barrier, len(plane + row_of_chips))
    m1_one(0)
    product(0, 0, 1, 1)
    m1_one(1)
    product(0, 0, 2)
    m1(1, 0)
    relayout(3, 0)
    product(3, 0, 2)
    first_pair()
    m2_up(1, 0)
    m2_down(1, 0)
    relayout(1, 1)
    product(1, 1, 0)
    m3_up(1, 0)
    m3_down(1, 0)
    product(1, 1, 2)
    m1(1, 1)
    m2_up(0, 0)
    relayout(2, 1)
    product(2, 1, 0)
    m2_down(0, 0)
    m2_up(1, 1)
    m2_down(1, 1)
    product(2, 1, 2)
    ring_end(1, 0)
    m3_up(0, 0)
    m3_down(0, 0)
    product(3, 0, 0)
    m3_up(1, 1)
    m3_down(1, 1)
    m2_up(0, 1)
    m2_down(0, 1)
    ladder_part(0)
    m1(1, 2)
    ladder_part(1)
    m3_up(0, 1)
    m3_down(0, 1)
    ladder_part(2)
    ring_end(0, 0)
    m2_up(1, 2)
    m2_down(1, 2)
    ladder_part(3)
    ladder_lanes()
    m2_up(0, 2)
    m2_down(0, 2)
    ring_end(1, 1)
    first_pair_end()
    m1(1, 3)
    late0(1)
    m3_up(1, 2)
    m3_down(1, 2)
    ring_end(0, 1)
    m3_up(0, 2)
    m3_down(0, 2)
    late0(0)
    m2_up(0, 3)
    m2_down(0, 3)
    m2_up(0, 4)
    m2_down(0, 4)
    late1(1)
    m3_up(0, 3)
    m3_down(0, 3)
    ring_end(1, 2)
    m2_up(1, 3)
    m2_down(1, 3)
    m3_up(1, 3)
    m3_down(1, 3)
    m3_up(0, 4)
    m3_down(0, 4)
    late1(0)
    ring_end(0, 2)
    ladder_plane()
    late2(1)
    late2(0)
    for name in ("itg", "his", "vir", "of", "os"):
        loads[name].wait()
    ring_end(0, 3)
    ring_end(0, 4)
    ring_end(1, 3)
    rows = ladder_end()
    late3(1)
    sums = tail(1, rows, [jnp.zeros((8, 128), F32)] * 6)
    late3(0)
    sums = tail(0, rows, sums)

    lane = lax.broadcasted_iota(jnp.int32, (1, 128), 1)
    mine = jnp.zeros((1, 128), F32)
    for n, s in enumerate(sums):
        one = jnp.sum(jnp.sum(s, axis=0, keepdims=True), axis=1, keepdims=True)
        mine = jnp.where(lane == n, one, mine)

    def everyone(buf, own, row, devices, n):
        count = len(devices)
        buf[own] = row
        for device in devices:
            pltpu.make_async_remote_copy(
                src_ref=buf.at[own], dst_ref=buf.at[own], send_sem=ss.at[n], recv_sem=qs.at[n],
                device_id=device, device_id_type=MESH,
            ).start()
        arrived = pltpu.make_async_remote_copy(
            src_ref=buf.at[pl.ds(0, count)], dst_ref=buf.at[pl.ds(0, count)], send_sem=ss.at[n], recv_sem=qs.at[n],
            device_id=devices[0], device_id_type=MESH,
        )
        arrived.wait_recv()
        return jnp.sum(buf[...], axis=0), arrived

    def totals():
        row, first = everyone(sums_a, z * 4 + y, mine, plane, 0)
        row, second = everyone(sums_b, xpos * 2 + core, row, row_of_chips, 1)
        tot_ref[...] = row * (1.0 / 8388608.0)
        first.wait_send()
        second.wait_send()

    totals()
    arrivals(lrecv_a, 0).wait_send()
    arrivals(lrecv_b, 1).wait_send()
    all_sent()


def shards(amplitudes, cycle_amps, cycle_ints, ladder_ints, integrals, history, vir_energy, occ_first, occ_second):
    bf16 = jnp.bfloat16
    dma = pltpu.SemaphoreType.DMA
    block = pltpu.VMEM((2, NI, NJ, 32, 256), F32)
    vmem = pl.BlockSpec(memory_space=pltpu.VMEM)
    stacked, totals = pl.pallas_call(
        kernel,
        out_shape=(block, pltpu.VMEM((1, 128), F32)),
        in_specs=[pl.BlockSpec(memory_space=pltpu.HBM)] * 9,
        out_specs=(vmem, vmem),
        scratch_shapes=[
            pltpu.VMEM((4, DEPTH, 4, 256), bf16),
            pltpu.VMEM((NI, DEPTH, 256), bf16),
            pltpu.VMEM((2, 4, DEPTH, 256), bf16),
            pltpu.VMEM((NJ, NI, 4, 2, 4, 32, 256), F32),
            pltpu.VMEM((2, 2, 2, 4, 32, 256), F32),
            pltpu.VMEM((2, 6, 4, 2, 2, 32, 256), F32),
            pltpu.VMEM((2, 4, 2, 2, 32, 256), F32),
            pltpu.VMEM((2, 2, 4, 32, 256), F32),
            pltpu.VMEM((2, 6, 2, 32, 256), F32),
            pltpu.VMEM((64, 4, 32, 256), bf16),
            pltpu.VMEM((4, 64, 256), F32),
            pltpu.VMEM((4, 4, 2, 8, 128), F32),
            pltpu.VMEM((7, 4, 8, 128), F32),
            pltpu.VMEM((4, 8, 128), F32),
            pltpu.VMEM((15, 8, 128), F32),
            pltpu.VMEM((NI, NJ, 32, 256), F32),
            pltpu.VMEM((NI, NJ, 32, 256), F32),
            pltpu.VMEM((4, NI, NJ, 32, 256), F32),
            pltpu.VMEM((1, 1024), F32),
            pltpu.VMEM((1, NI), F32),
            pltpu.VMEM((1, NJ), F32),
            pltpu.VMEM((16, 1, 128), F32),
            pltpu.VMEM((8, 1, 128), F32),
            dma((17,)),
            dma((9,)),
            dma((2,)),
            dma((2, 4)),
            dma((2, 5)),
            dma((2, 5)),
            dma((2, 3)),
            dma((1,)),
            dma((2,)), dma((2,)),
            dma((2,)), dma((2,)),
        ],
        compiler_params=pltpu.CompilerParams(
            collective_id=0, has_side_effects=True, vmem_limit_bytes=52 * 2**20
        ),
        cost_estimate=pl.CostEstimate(flops=9 * 10**9, bytes_accessed=27 * 10**6, transcendentals=0),
        name="window",
    )(*(pltpu.with_memory_space_constraint(x, pltpu.HBM) for x in (
        amplitudes,
        cycle_amps.reshape(NI, DEPTH, 256),
        cycle_ints.reshape(DEPTH, 4, 1024),
        ladder_ints,
        integrals,
        history,
        vir_energy.reshape(1, 1024),
        occ_first.reshape(1, NI),
        occ_second.reshape(1, NJ),
    )))
    return stacked[0], stacked[1], totals[0, :1], totals[0, 1:6]


def solution(mesh):
    spread = P(None, None, "wide", "narrow")
    return jax.shard_map(
        shards,
        mesh=mesh,
        in_specs=(
            spread,
            spread,
            P(None, "wide", None, None),
            spread,
            spread,
            P(None, None, None, "wide", "narrow"),
            P(),
            P(),
            P(),
        ),
        out_specs=(spread, spread, P(), P()),
        check_vma=False,
    )
```

```python
import jax
import jax.numpy as jnp
from jax import lax
from jax.experimental import pallas as pl
from jax.experimental.pallas import tpu as pltpu
from jax.sharding import PartitionSpec as P

NI = 2
NJ = 4
DEPTH = 2048
MESH = pl.DeviceIdType.MESH
CHUNKS = (2, 1, 3, 0)
F32 = jnp.float32


def kernel(
    amp_hbm, u_hbm, m_hbm, lad_hbm, itg_hbm, his_hbm, vir_hbm, of_hbm, os_hbm,
    both_ref, tot_ref,
    mbuf, ubuf, wbuf, part, r0, r1, rx, rf, rg, r3,
    lbuf, lgrp, lsum, lrecv_a, lplane, lrecv_b,
    amp, itg, his, vir, of_ref, os_ref, sums_a, sums_b,
    lsem, sent, q0, q1, qe, qx, q3, qf, sl, ql, ss, qs,
):
    wide = lax.axis_index("wide")
    narrow = lax.axis_index("narrow")
    z = wide // 8
    xh = lax.rem(wide // 4, 2)
    y = lax.rem(wide, 4)
    xl = narrow // 2
    core = lax.rem(narrow, 2)
    xpos = xh * 2 + xl

    def at(z_, y_, x_, core_):
        return {
            "wide": lax.rem(z_, 4) * 8 + lax.rem(x_, 4) // 2 * 4 + lax.rem(y_, 4),
            "narrow": lax.rem(x_, 2) * 2 + lax.rem(core_, 2),
        }

    def along(axis, delta):
        if axis == "z":
            return at(z + delta, y, xpos, core)
        if axis == "y":
            return at(z, y + delta, xpos, core)
        return at(z, y, xpos + delta, core)

    barrier = pltpu.get_barrier_semaphore()
    plane = [at(z + d // 4, y + d % 4, xpos, core) for d in range(1, 16)]
    row_of_chips = [at(z, y, xpos + d // 2, core + d % 2) for d in range(1, 8)]
    for device in plane + row_of_chips:
        pl.semaphore_signal(barrier, inc=1, device_id=device, device_id_type=MESH)

    loads = {}

    def load(name, src, dst, n):
        loads[name] = pltpu.make_async_copy(src, dst, lsem.at[n])
        loads[name].start()

    def columns(c, x0, width):
        zc = lax.rem(z + CHUNKS[c], 4)
        return pl.ds(pl.multiple_of(zc * 256 + x0, 128), width)

    for q in range(4):
        rows_q = pl.ds(q * (DEPTH // 4), DEPTH // 4)
        load(("q", q), m_hbm.at[rows_q, :, columns(0, 0, 256)], mbuf.at[0, rows_q], 12 + q)
    load("u", u_hbm, ubuf, 0)

    def load_rest():
        for c in (3, 1, 2):
            load(("m", c), m_hbm.at[:, :, columns(c, 0, 256)], mbuf.at[c], 1 + c)
        load("amp", amp_hbm, amp, 5)
        load("lad", lad_hbm, lbuf, 6)
        load("itg", itg_hbm, itg, 7)
        load("his", his_hbm, his, 8)
        load("vir", vir_hbm, vir, 9)
        load("of", of_hbm, of_ref, 1)
        load("os", os_hbm, os_ref, 16)

    def send(src, dst, group, rsem, device):
        pltpu.make_async_remote_copy(
            src_ref=src, dst_ref=dst, send_sem=sent.at[group], recv_sem=rsem, device_id=device, device_id_type=MESH
        ).start()

    def all_sent():
        rings = [
            ref
            for cls, kinds in ((0, pl.ds(2, 4)), (1, pl.ds(0, 6)))
            for ref in (r1.at[cls, kinds, pl.ds(0, 3)], r1.at[cls, kinds, 3, pl.ds(0, 1)], r1.at[cls, kinds, 3, pl.ds(1, 1), 0])
        ]
        pairs = [ref for cls in range(2) for ref in (rx.at[cls, pl.ds(0, 3)], rx.at[cls, 3, pl.ds(0, 1)])]
        groups = [r0, *rings, *pairs, rf, rg, r3.at[0], r3.at[1]]
        for group, ref in enumerate(groups):
            pltpu.make_async_remote_copy(
                src_ref=ref, dst_ref=ref, send_sem=sent.at[group], recv_sem=q0.at[0], device_id=plane[0],
                device_id_type=MESH,
            ).wait_send()

    ring_axis = ("z", "y")
    ring_pos = (z, y)
    chunk_pos = (y, z)

    def places(cls, ring_offset, c):
        ring = lax.rem(ring_pos[cls] + ring_offset, 4)
        chunk = lax.rem(chunk_pos[cls] + CHUNKS[min(c, 3)], 4)
        return (ring, chunk) if cls == 0 else (chunk, ring)

    def js(cls, c):
        return pl.ds(2 * cls + c - 3, 1) if c >= 3 else pl.ds(2 * cls, 2)

    def x_first(cls, c):
        return c == 4

    def whole(cls, i, ring_offset, c):
        zp, yp = places(cls, ring_offset, c)
        return part.at[js(cls, c), i, zp, xh if x_first(cls, c) else slice(None), yp]

    def landing(cls, kind, c):
        if c < 3:
            return r1.at[cls, kind, c]
        place = r1.at[cls, kind, 3, pl.ds(c - 3, 1)]
        return place.at[:, 0] if x_first(cls, c) else place

    def wait_bytes(ref, sem):
        pltpu.make_async_remote_copy(
            src_ref=ref, dst_ref=ref, send_sem=sent.at[0], recv_sem=sem, device_id=plane[0], device_id_type=MESH
        ).wait_recv()

    def first_pair():
        send(part.at[3, :, z, 1 - xh], rf, 11, qf.at[0], along("x", 2))

    def first_pair_end():
        wait_bytes(rf, qf.at[0])
        part[3, :, z, xh] += rf[...]

    def second_pair():
        early(0, 0, 4, True)
        early(0, 1, 4, True)
        for n, offset in enumerate((1, 3, 0)):
            send(part.at[1, :, lax.rem(z + offset, 4), 1 - xh, y], rg.at[n], 12, qf.at[1], along("x", 2))

    def second_pair_end():
        wait_bytes(rg, qf.at[1])
        for n, offset in enumerate((1, 3, 0)):
            part[1, :, lax.rem(z + offset, 4), xh, y] += rg[n]

    def ring_send(cls, kind, c, i, ring_offset, step):
        group = 1 + 3 * cls + max(c - 2, 0)
        send(whole(cls, i, ring_offset, c), landing(cls, kind, c), group,
             q1.at[kind, c] if kind < 2 else qe.at[cls, c], along(ring_axis[cls], step))

    def m1(cls, c):
        ring_send(cls, 0, c, 0, 2, 1)
        ring_send(cls, 1, c, 1, 2, 3)

    def m1_one(j):
        zp = lax.rem(z + 2, 4)
        for i, step in ((0, 1), (1, 3)):
            send(part.at[j, i, zp], r0.at[i, j], 0, q0.at[i], along("z", step))

    def early(cls, i, c, now=False):
        if cls == 0 and x_first(cls, c):
            if now:
                part[1, i, lax.rem(z + 1 + 2 * i, 4), :, y] += r0[i, 1, :, y]
            return
        ref = whole(cls, i, 1 + 2 * i, c)
        if cls == 1:
            wait_bytes(landing(cls, i, c), q1.at[i, c])
            ref[...] += landing(cls, i, c)[...]
            return
        if c == 0:
            wait_bytes(r0.at[i], q0.at[i])
        ref[...] += r0[i, js(cls, c), :, places(cls, 0, c)[1]]

    def m2_up(cls, c):
        ring_send(cls, 2, c, 1, 1, 1)

    def m2_down(cls, c):
        ring_send(cls, 3, c, 0, 3, 3)

    def m3_up(cls, c):
        early(cls, 0, c)
        ring_send(cls, 4, c, 0, 1, 1)

    def m3_down(cls, c):
        early(cls, 1, c)
        ring_send(cls, 5, c, 1, 3, 3)

    def ring_end(cls, c):
        if c < 3:
            wait_bytes(r1.at[cls, pl.ds(2, 4), c], qe.at[cls, c])
        elif c == 3:
            wait_bytes(r1.at[cls, pl.ds(2, 4), 3, pl.ds(0, 1)], qe.at[cls, c])
        else:
            wait_bytes(r1.at[cls, pl.ds(2, 4), 3, pl.ds(1, 1), 0], qe.at[cls, c])
        first = whole(cls, 0, 0, c)
        first[...] += landing(cls, 4, c)[...] + landing(cls, 3, c)[...]
        second = whole(cls, 1, 0, c)
        second[...] += landing(cls, 2, c)[...] + landing(cls, 5, c)[...]
        if x_first(cls, c):
            return
        zp, yp = places(cls, 0, c)
        send(part.at[js(cls, c), :, zp, 1 - xh, yp], paired(cls, c), 7 + 2 * cls + (c == 3), qx.at[cls, c], along("x", 2))

    def paired(cls, c):
        return rx.at[cls, 3, pl.ds(0, 1)] if c == 3 else rx.at[cls, c]

    def pair_end(cls, c):
        if x_first(cls, c):
            return
        wait_bytes(paired(cls, c), qx.at[cls, c])
        zp, yp = places(cls, 0, c)
        ref = part.at[js(cls, c), :, zp, xh, yp]
        ref[...] += paired(cls, c)[...]

    def own_x(cls, i, c):
        zp, yp = places(cls, 0, c)
        return part.at[pl.ds(2 * cls, 2), i, zp, xh, yp]

    def late_send(cls, kind, c, i, step):
        send(own_x(cls, i, c), r3.at[cls, kind], 13 + cls, q3.at[cls, min(kind, 2)], along(ring_axis[1 - cls], step))

    def late0(cls):
        pair_end(cls, 0)
        late_send(cls, 0, 0, 0, 1)
        late_send(cls, 1, 0, 1, 3)

    def late1(cls):
        pair_end(cls, 1)
        late_send(cls, 2, 1, 1, 1)
        wait_bytes(r3.at[cls, 0], q3.at[cls, 0])
        ref = own_x(cls, 0, 1)
        ref[...] += r3[cls, 0]
        late_send(cls, 4, 1, 0, 1)

    def late2(cls):
        pair_end(cls, 2)
        late_send(cls, 3, 2, 0, 3)
        wait_bytes(r3.at[cls, 1], q3.at[cls, 1])
        ref = own_x(cls, 1, 2)
        ref[...] += r3[cls, 1]
        late_send(cls, 5, 2, 1, 3)

    def late3(cls):
        wait_bytes(r3.at[cls, pl.ds(2, 4)], q3.at[cls, 2])
        pair_end(cls, 3)
        first = own_x(cls, 0, 3)
        first[...] += r3[cls, 4] + r3[cls, 3]
        second = own_x(cls, 1, 3)
        second[...] += r3[cls, 2] + r3[cls, 5]

    def relayout(c, b):
        def body(t, carry):
            k0 = pl.multiple_of(t * 64, 64)
            wbuf[b, :, pl.ds(k0, 64), :] = jnp.swapaxes(mbuf[c, pl.ds(k0, 64)], 0, 1)
            return carry

        steps = DEPTH // 64
        if c:
            loads["m", c].wait()
            lax.fori_loop(0, steps, body, 0)
            return
        for q in range(4):
            loads["q", q].wait()
            lax.fori_loop(q * steps // 4, (q + 1) * steps // 4, body, 0)

    def product(c, b, first, count=2):
        zp = lax.rem(z + CHUNKS[c], 4)

        def body(j, carry):
            for i in range(NI):
                got = lax.dot_general(wbuf[b, j], ubuf[i], (((0,), (0,)), ((), ())), preferred_element_type=F32)
                part[j, i, zp] = got.reshape(2, 4, 32, 256)
            return carry

        lax.fori_loop(first, first + count, body, 0)

    def ladder_part(s):
        if s == 0:
            loads["amp"].wait()
            loads["lad"].wait()
        rounded = amp[...].reshape(256, 256).astype(jnp.bfloat16)
        row = lax.broadcasted_iota(jnp.int32, (32, 256), 0)
        lane = lax.broadcasted_iota(jnp.int32, (32, 256), 1)
        same = jnp.where(lax.rem(lane, 32) == row, 1.0, 0.0).astype(F32)

        def body(t, carry):
            r0_ = pl.multiple_of(t * 16, 16)
            ints = lbuf[pl.ds(r0_, 16), s].reshape(512, 256)
            full = lax.dot_general(ints, rounded, (((1,), (1,)), ((), ())), preferred_element_type=F32)
            lgrp[s, pl.ds(r0_, 16), :] = jnp.sum(full.reshape(16, 32, 256) * same[None], axis=1)
            return carry

        lax.fori_loop(0, 4, body, 0)

    def ladder_lanes():
        group = lax.broadcasted_iota(jnp.int32, (256, 128), 0) // 32
        slot = lax.broadcasted_iota(jnp.int32, (256, 128), 1)
        pick = jnp.where(group == slot, 1.0, 0.0).astype(F32)
        lsum[...] = jnp.dot(
            lgrp[...].reshape(256, 256), pick, precision=lax.Precision.HIGHEST, preferred_element_type=F32
        ).reshape(4, 4, 2, 8, 128)
        for d in range(1, 8):
            xd = lax.rem(xpos + d // 2, 4)
            cd = lax.rem(core + d % 2, 2)
            pltpu.make_async_remote_copy(
                src_ref=lsum.at[lax.rem(xd, 2) * 2 + cd, :, xd // 2], dst_ref=lrecv_a.at[d - 1],
                send_sem=sl.at[0], recv_sem=ql.at[0], device_id=at(z, y, xd, cd), device_id_type=MESH,
            ).start()

    def arrivals(ref, n):
        return pltpu.make_async_remote_copy(
            src_ref=ref, dst_ref=ref, send_sem=sl.at[n], recv_sem=ql.at[n], device_id=plane[0], device_id_type=MESH
        )

    def ladder_plane():
        arrivals(lrecv_a, 0).wait_recv()
        lplane[...] = lsum[narrow, :, xh] + jnp.sum(lrecv_a[...], axis=0)
        for d in range(1, 16):
            pltpu.make_async_remote_copy(
                src_ref=lplane.at[lax.rem(z + d // 4, 4)], dst_ref=lrecv_b.at[d - 1],
                send_sem=sl.at[1], recv_sem=ql.at[1], device_id=plane[d - 1], device_id_type=MESH,
            ).start()

    def ladder_end():
        arrivals(lrecv_b, 1).wait_recv()
        total = lplane[z] + jnp.sum(lrecv_b[...], axis=0)
        row = lax.broadcasted_iota(jnp.int32, (8, 128), 0)
        return [jnp.sum(jnp.where(row == 2 * y + e, total, 0.0), axis=0, keepdims=True) for e in range(2)]

    def fold(x):
        eight = jnp.sum(x.reshape(4, 8, 256), axis=0)
        return eight[:, :128] + eight[:, 128:]

    def tail(cls, ladder_rows, sums):
        row = lax.broadcasted_iota(jnp.int32, (32, 256), 0)
        lane = lax.broadcasted_iota(jnp.int32, (32, 256), 1)
        lane1 = lax.broadcasted_iota(jnp.int32, (1, 128), 1)
        lanes = lax.broadcasted_iota(jnp.int32, (32, 128), 1)
        rows = lax.broadcasted_iota(jnp.int32, (32, 128), 0)
        block = vir[:, pl.ds(pl.multiple_of(wide // 4 * 128, 128), 128)]
        down = jnp.sum(jnp.where(lanes == lax.rem(wide, 4) * 32 + rows, block, 0.0), axis=1, keepdims=True)
        across = vir[:, pl.ds(pl.multiple_of(narrow * 256, 256), 256)]
        for j in (2 * cls, 2 * cls + 1):
            for i in range(NI):
                ij = i * NJ + j
                placed = jnp.zeros((32, 256), F32)
                for e in range(2):
                    one = jnp.sum(jnp.where(lane1 == ij, ladder_rows[e], 0.0), axis=1, keepdims=True)
                    placed = jnp.where((row == e) & (lane == 0), one, placed)
                denominator = down + across - of_ref[:, i : i + 1] - os_ref[:, j : j + 1]
                a = amp[i, j]
                v = itg[i, j]
                r = v + part[j, i, z, xh, y] + placed - denominator * a
                new = a + r / denominator
                both_ref[1, i, j] = r
                both_ref[0, i, j] = new
                terms = [new * v] + [his[h, i, j] * r for h in range(4)] + [r * r]
                sums = [s + fold(t) for s, t in zip(sums, terms)]
        return sums

    relayout(0, 0)
    loads["u"].wait()
    load_rest()
    product(0, 0, 0, 1)
    pl.semaphore_wait(barrier, len(plane + row_of_chips))
    m1_one(0)
    product(0, 0, 1, 1)
    m1_one(1)
    product(0, 0, 2)
    m1(1, 0)
    relayout(3, 0)
    product(3, 0, 2)
    first_pair()
    m2_up(1, 0)
    m2_down(1, 0)
    relayout(1, 1)
    product(1, 1, 0)
    m3_up(1, 0)
    m3_down(1, 0)
    product(1, 1, 2)
    m1(1, 1)
    m2_up(0, 0)
    relayout(2, 1)
    product(2, 1, 0)
    m2_down(0, 0)
    m2_up(1, 1)
    m2_down(1, 1)
    product(2, 1, 2)
    ring_end(1, 0)
    m1(1, 2)
    m3_up(0, 0)
    m3_down(0, 0)
    product(3, 0, 0)
    m3_up(1, 1)
    m3_down(1, 1)
    m2_up(0, 1)
    m2_down(0, 1)
    second_pair()
    ladder_part(0)
    ladder_part(1)
    m3_up(0, 1)
    m3_down(0, 1)
    ladder_part(2)
    ring_end(0, 0)
    m2_up(1, 2)
    m2_down(1, 2)
    ladder_part(3)
    ladder_lanes()
    m2_up(0, 2)
    m2_down(0, 2)
    ring_end(1, 1)
    m3_up(1, 2)
    m3_down(1, 2)
    first_pair_end()
    m1(1, 3)
    m1(1, 4)
    late0(1)
    ring_end(0, 1)
    m3_up(0, 2)
    m3_down(0, 2)
    late0(0)
    m2_up(0, 3)
    m2_down(0, 3)
    ring_end(1, 2)
    m2_up(1, 3)
    m2_down(1, 3)
    late1(1)
    ladder_plane()
    second_pair_end()
    m3_up(0, 3)
    m3_down(0, 3)
    m2_up(0, 4)
    m2_down(0, 4)
    m3_up(1, 3)
    m3_down(1, 3)
    m3_up(0, 4)
    m3_down(0, 4)
    ring_end(0, 2)
    late1(0)
    m2_up(1, 4)
    m2_down(1, 4)
    m3_up(1, 4)
    m3_down(1, 4)
    late2(1)
    late2(0)
    for name in ("itg", "his", "vir", "of", "os"):
        loads[name].wait()
    ring_end(1, 3)
    ring_end(0, 3)
    ring_end(0, 4)
    ring_end(1, 4)
    rows = ladder_end()
    late3(1)
    sums = tail(1, rows, [jnp.zeros((8, 128), F32)] * 6)
    late3(0)
    sums = tail(0, rows, sums)

    lane = lax.broadcasted_iota(jnp.int32, (1, 128), 1)
    mine = jnp.zeros((1, 128), F32)
    for n, s in enumerate(sums):
        one = jnp.sum(jnp.sum(s, axis=0, keepdims=True), axis=1, keepdims=True)
        mine = jnp.where(lane == n, one, mine)

    def everyone(buf, own, row, devices, n):
        count = len(devices)
        buf[own] = row
        for device in devices:
            pltpu.make_async_remote_copy(
                src_ref=buf.at[own], dst_ref=buf.at[own], send_sem=ss.at[n], recv_sem=qs.at[n],
                device_id=device, device_id_type=MESH,
            ).start()
        arrived = pltpu.make_async_remote_copy(
            src_ref=buf.at[pl.ds(0, count)], dst_ref=buf.at[pl.ds(0, count)], send_sem=ss.at[n], recv_sem=qs.at[n],
            device_id=devices[0], device_id_type=MESH,
        )
        arrived.wait_recv()
        return jnp.sum(buf[...], axis=0), arrived

    def totals():
        row, first = everyone(sums_a, z * 4 + y, mine, plane, 0)
        row, second = everyone(sums_b, xpos * 2 + core, row, row_of_chips, 1)
        tot_ref[...] = row * (1.0 / 8388608.0)
        first.wait_send()
        second.wait_send()

    totals()
    arrivals(lrecv_a, 0).wait_send()
    arrivals(lrecv_b, 1).wait_send()
    all_sent()


def shards(amplitudes, cycle_amps, cycle_ints, ladder_ints, integrals, history, vir_energy, occ_first, occ_second):
    bf16 = jnp.bfloat16
    dma = pltpu.SemaphoreType.DMA
    block = pltpu.VMEM((2, NI, NJ, 32, 256), F32)
    vmem = pl.BlockSpec(memory_space=pltpu.VMEM)
    stacked, totals = pl.pallas_call(
        kernel,
        out_shape=(block, pltpu.VMEM((1, 128), F32)),
        in_specs=[pl.BlockSpec(memory_space=pltpu.HBM)] * 9,
        out_specs=(vmem, vmem),
        scratch_shapes=[
            pltpu.VMEM((4, DEPTH, 4, 256), bf16),
            pltpu.VMEM((NI, DEPTH, 256), bf16),
            pltpu.VMEM((2, 4, DEPTH, 256), bf16),
            pltpu.VMEM((NJ, NI, 4, 2, 4, 32, 256), F32),
            pltpu.VMEM((2, 2, 2, 4, 32, 256), F32),
            pltpu.VMEM((2, 6, 4, 2, 2, 32, 256), F32),
            pltpu.VMEM((2, 4, 2, 2, 32, 256), F32),
            pltpu.VMEM((2, 4, 32, 256), F32),
            pltpu.VMEM((3, 2, 32, 256), F32),
            pltpu.VMEM((2, 6, 2, 32, 256), F32),
            pltpu.VMEM((64, 4, 32, 256), bf16),
            pltpu.VMEM((4, 64, 256), F32),
            pltpu.VMEM((4, 4, 2, 8, 128), F32),
            pltpu.VMEM((7, 4, 8, 128), F32),
            pltpu.VMEM((4, 8, 128), F32),
            pltpu.VMEM((15, 8, 128), F32),
            pltpu.VMEM((NI, NJ, 32, 256), F32),
            pltpu.VMEM((NI, NJ, 32, 256), F32),
            pltpu.VMEM((4, NI, NJ, 32, 256), F32),
            pltpu.VMEM((1, 1024), F32),
            pltpu.VMEM((1, NI), F32),
            pltpu.VMEM((1, NJ), F32),
            pltpu.VMEM((16, 1, 128), F32),
            pltpu.VMEM((8, 1, 128), F32),
            dma((17,)),
            dma((15,)),
            dma((2,)),
            dma((2, 5)),
            dma((2, 5)),
            dma((2, 5)),
            dma((2, 3)),
            dma((2,)),
            dma((2,)), dma((2,)),
            dma((2,)), dma((2,)),
        ],
        compiler_params=pltpu.CompilerParams(
            collective_id=0, has_side_effects=True, vmem_limit_bytes=52 * 2**20
        ),
        cost_estimate=pl.CostEstimate(flops=9 * 10**9, bytes_accessed=27 * 10**6, transcendentals=0),
        name="window",
    )(*(pltpu.with_memory_space_constraint(x, pltpu.HBM) for x in (
        amplitudes,
        cycle_amps.reshape(NI, DEPTH, 256),
        cycle_ints.reshape(DEPTH, 4, 1024),
        ladder_ints,
        integrals,
        history,
        vir_energy.reshape(1, 1024),
        occ_first.reshape(1, NI),
        occ_second.reshape(1, NJ),
    )))
    return stacked[0], stacked[1], totals[0, :1], totals[0, 1:6]


def solution(mesh):
    spread = P(None, None, "wide", "narrow")
    return jax.shard_map(
        shards,
        mesh=mesh,
        in_specs=(
            spread,
            spread,
            P(None, "wide", None, None),
            spread,
            spread,
            P(None, None, None, "wide", "narrow"),
            P(),
            P(),
            P(),
        ),
        out_specs=(spread, spread, P(), P()),
        check_vma=False,
    )
```

```python
import jax
import jax.numpy as jnp
from jax import lax
from jax.experimental import pallas as pl
from jax.experimental.pallas import tpu as pltpu
from jax.sharding import PartitionSpec as P

NI = 2
NJ = 4
DEPTH = 2048
MESH = pl.DeviceIdType.MESH
CHUNKS = (2, 1, 3, 0)
F32 = jnp.float32


def kernel(
    amp_hbm, u_hbm, m_hbm, lad_hbm, itg_hbm, his_hbm, vir_hbm, of_hbm, os_hbm,
    both_ref, tot_ref,
    mbuf, ubuf, wbuf, part, r0, r1, rx, rf, rg, r3,
    lbuf, lgrp, lsum, lrecv_a, lplane, lrecv_b,
    amp, itg, his, vir, of_ref, os_ref, sums_a,
    lsem, sent, q0, q1, qe, qx, q3, qf, sl, ql, ss, qs,
):
    wide = lax.axis_index("wide")
    narrow = lax.axis_index("narrow")
    z = wide // 8
    xh = lax.rem(wide // 4, 2)
    y = lax.rem(wide, 4)
    xl = narrow // 2
    core = lax.rem(narrow, 2)
    xpos = xh * 2 + xl

    def at(z_, y_, x_, core_):
        return {
            "wide": lax.rem(z_, 4) * 8 + lax.rem(x_, 4) // 2 * 4 + lax.rem(y_, 4),
            "narrow": lax.rem(x_, 2) * 2 + lax.rem(core_, 2),
        }

    def along(axis, delta):
        if axis == "z":
            return at(z + delta, y, xpos, core)
        if axis == "y":
            return at(z, y + delta, xpos, core)
        return at(z, y, xpos + delta, core)

    barrier = pltpu.get_barrier_semaphore()
    plane = [at(z + d // 4, y + d % 4, xpos, core) for d in range(1, 16)]
    row_of_chips = [at(z, y, xpos + d // 2, core + d % 2) for d in range(1, 8)]
    for device in plane + row_of_chips:
        pl.semaphore_signal(barrier, inc=1, device_id=device, device_id_type=MESH)

    loads = {}

    def load(name, src, dst, n):
        loads[name] = pltpu.make_async_copy(src, dst, lsem.at[n])
        loads[name].start()

    def columns(c, x0, width):
        zc = lax.rem(z + CHUNKS[c], 4)
        return pl.ds(pl.multiple_of(zc * 256 + x0, 128), width)

    for q in range(4):
        rows_q = pl.ds(q * (DEPTH // 4), DEPTH // 4)
        load(("q", q), m_hbm.at[rows_q, :, columns(0, 0, 256)], mbuf.at[0, rows_q], 12 + q)
    load("u", u_hbm, ubuf, 0)

    def load_rest():
        for c in (3, 1, 2):
            load(("m", c), m_hbm.at[:, :, columns(c, 0, 256)], mbuf.at[c], 1 + c)
        load("amp", amp_hbm, amp, 5)
        load("lad", lad_hbm, lbuf, 6)
        load("itg", itg_hbm, itg, 7)
        load("his", his_hbm, his, 8)
        load("vir", vir_hbm, vir, 9)
        load("of", of_hbm, of_ref, 1)
        load("os", os_hbm, os_ref, 16)

    def send(src, dst, group, rsem, device):
        pltpu.make_async_remote_copy(
            src_ref=src, dst_ref=dst, send_sem=sent.at[group], recv_sem=rsem, device_id=device, device_id_type=MESH
        ).start()

    def all_sent():
        rings = [
            ref
            for cls, kinds in ((0, pl.ds(2, 4)), (1, pl.ds(0, 6)))
            for ref in (r1.at[cls, kinds, pl.ds(0, 3)], r1.at[cls, kinds, 3, pl.ds(0, 1)], r1.at[cls, kinds, 3, pl.ds(1, 1), 0])
        ]
        pairs = [ref for cls in range(2) for ref in (rx.at[cls, pl.ds(0, 3)], rx.at[cls, 3, pl.ds(0, 1)])]
        groups = [r0, *rings, *pairs, rf, rg, r3.at[0], r3.at[1]]
        for group, ref in enumerate(groups):
            pltpu.make_async_remote_copy(
                src_ref=ref, dst_ref=ref, send_sem=sent.at[group], recv_sem=q0.at[0], device_id=plane[0],
                device_id_type=MESH,
            ).wait_send()

    ring_axis = ("z", "y")
    ring_pos = (z, y)
    chunk_pos = (y, z)

    def places(cls, ring_offset, c):
        ring = lax.rem(ring_pos[cls] + ring_offset, 4)
        chunk = lax.rem(chunk_pos[cls] + CHUNKS[min(c, 3)], 4)
        return (ring, chunk) if cls == 0 else (chunk, ring)

    def js(cls, c):
        return pl.ds(2 * cls + c - 3, 1) if c >= 3 else pl.ds(2 * cls, 2)

    def x_first(cls, c):
        return c == 4

    def whole(cls, i, ring_offset, c):
        zp, yp = places(cls, ring_offset, c)
        return part.at[js(cls, c), i, zp, xh if x_first(cls, c) else slice(None), yp]

    def landing(cls, kind, c):
        if c < 3:
            return r1.at[cls, kind, c]
        place = r1.at[cls, kind, 3, pl.ds(c - 3, 1)]
        return place.at[:, 0] if x_first(cls, c) else place

    def wait_bytes(ref, sem):
        pltpu.make_async_remote_copy(
            src_ref=ref, dst_ref=ref, send_sem=sent.at[0], recv_sem=sem, device_id=plane[0], device_id_type=MESH
        ).wait_recv()

    def first_pair():
        send(part.at[3, :, z, 1 - xh], rf, 11, qf.at[0], along("x", 2))

    def first_pair_end():
        wait_bytes(rf, qf.at[0])
        part[3, :, z, xh] += rf[...]

    def second_pair():
        early(0, 0, 4, True)
        early(0, 1, 4, True)
        for n, offset in enumerate((1, 3, 0)):
            send(part.at[1, :, lax.rem(z + offset, 4), 1 - xh, y], rg.at[n], 12, qf.at[1], along("x", 2))

    def second_pair_end():
        wait_bytes(rg, qf.at[1])
        for n, offset in enumerate((1, 3, 0)):
            part[1, :, lax.rem(z + offset, 4), xh, y] += rg[n]

    def ring_send(cls, kind, c, i, ring_offset, step):
        group = 1 + 3 * cls + max(c - 2, 0)
        send(whole(cls, i, ring_offset, c), landing(cls, kind, c), group,
             q1.at[kind, c] if kind < 2 else qe.at[cls, c], along(ring_axis[cls], step))

    def m1(cls, c):
        ring_send(cls, 0, c, 0, 2, 1)
        ring_send(cls, 1, c, 1, 2, 3)

    def m1_one(j):
        zp = lax.rem(z + 2, 4)
        for i, step in ((0, 1), (1, 3)):
            send(part.at[j, i, zp], r0.at[i, j], 0, q0.at[i], along("z", step))

    def early(cls, i, c, now=False):
        if cls == 0 and x_first(cls, c):
            if now:
                part[1, i, lax.rem(z + 1 + 2 * i, 4), :, y] += r0[i, 1, :, y]
            return
        ref = whole(cls, i, 1 + 2 * i, c)
        if cls == 1:
            wait_bytes(landing(cls, i, c), q1.at[i, c])
            ref[...] += landing(cls, i, c)[...]
            return
        if c == 0:
            wait_bytes(r0.at[i], q0.at[i])
        ref[...] += r0[i, js(cls, c), :, places(cls, 0, c)[1]]

    def m2_up(cls, c):
        ring_send(cls, 2, c, 1, 1, 1)

    def m2_down(cls, c):
        ring_send(cls, 3, c, 0, 3, 3)

    def m3_up(cls, c):
        early(cls, 0, c)
        ring_send(cls, 4, c, 0, 1, 1)

    def m3_down(cls, c):
        early(cls, 1, c)
        ring_send(cls, 5, c, 1, 3, 3)

    def ring_end(cls, c):
        if c < 3:
            wait_bytes(r1.at[cls, pl.ds(2, 4), c], qe.at[cls, c])
        elif c == 3:
            wait_bytes(r1.at[cls, pl.ds(2, 4), 3, pl.ds(0, 1)], qe.at[cls, c])
        else:
            wait_bytes(r1.at[cls, pl.ds(2, 4), 3, pl.ds(1, 1), 0], qe.at[cls, c])
        first = whole(cls, 0, 0, c)
        first[...] += landing(cls, 4, c)[...] + landing(cls, 3, c)[...]
        second = whole(cls, 1, 0, c)
        second[...] += landing(cls, 2, c)[...] + landing(cls, 5, c)[...]
        if x_first(cls, c):
            return
        zp, yp = places(cls, 0, c)
        send(part.at[js(cls, c), :, zp, 1 - xh, yp], paired(cls, c), 7 + 2 * cls + (c == 3), qx.at[cls, c], along("x", 2))

    def paired(cls, c):
        return rx.at[cls, 3, pl.ds(0, 1)] if c == 3 else rx.at[cls, c]

    def pair_end(cls, c):
        if x_first(cls, c):
            return
        wait_bytes(paired(cls, c), qx.at[cls, c])
        zp, yp = places(cls, 0, c)
        ref = part.at[js(cls, c), :, zp, xh, yp]
        ref[...] += paired(cls, c)[...]

    def own_x(cls, i, c):
        zp, yp = places(cls, 0, c)
        return part.at[pl.ds(2 * cls, 2), i, zp, xh, yp]

    def late_send(cls, kind, c, i, step):
        send(own_x(cls, i, c), r3.at[cls, kind], 13 + cls, q3.at[cls, min(kind, 2)], along(ring_axis[1 - cls], step))

    def late0(cls):
        pair_end(cls, 0)
        late_send(cls, 0, 0, 0, 1)
        late_send(cls, 1, 0, 1, 3)

    def late1(cls):
        pair_end(cls, 1)
        late_send(cls, 2, 1, 1, 1)
        wait_bytes(r3.at[cls, 0], q3.at[cls, 0])
        ref = own_x(cls, 0, 1)
        ref[...] += r3[cls, 0]
        late_send(cls, 4, 1, 0, 1)

    def late2(cls):
        pair_end(cls, 2)
        late_send(cls, 3, 2, 0, 3)
        wait_bytes(r3.at[cls, 1], q3.at[cls, 1])
        ref = own_x(cls, 1, 2)
        ref[...] += r3[cls, 1]
        late_send(cls, 5, 2, 1, 3)

    def late3(cls):
        wait_bytes(r3.at[cls, pl.ds(2, 4)], q3.at[cls, 2])
        pair_end(cls, 3)
        first = own_x(cls, 0, 3)
        first[...] += r3[cls, 4] + r3[cls, 3]
        second = own_x(cls, 1, 3)
        second[...] += r3[cls, 2] + r3[cls, 5]

    def relayout(c, b):
        def body(t, carry):
            k0 = pl.multiple_of(t * 64, 64)
            wbuf[b, :, pl.ds(k0, 64), :] = jnp.swapaxes(mbuf[c, pl.ds(k0, 64)], 0, 1)
            return carry

        steps = DEPTH // 64
        if c:
            loads["m", c].wait()
            lax.fori_loop(0, steps, body, 0)
            return
        for q in range(4):
            loads["q", q].wait()
            lax.fori_loop(q * steps // 4, (q + 1) * steps // 4, body, 0)

    def product(c, b, first, count=2):
        zp = lax.rem(z + CHUNKS[c], 4)

        def body(j, carry):
            for i in range(NI):
                got = lax.dot_general(wbuf[b, j], ubuf[i], (((0,), (0,)), ((), ())), preferred_element_type=F32)
                part[j, i, zp] = got.reshape(2, 4, 32, 256)
            return carry

        lax.fori_loop(first, first + count, body, 0)

    def ladder_part(s):
        if s == 0:
            loads["amp"].wait()
            loads["lad"].wait()
        rounded = amp[...].reshape(256, 256).astype(jnp.bfloat16)
        row = lax.broadcasted_iota(jnp.int32, (32, 256), 0)
        lane = lax.broadcasted_iota(jnp.int32, (32, 256), 1)
        same = jnp.where(lax.rem(lane, 32) == row, 1.0, 0.0).astype(F32)

        def body(t, carry):
            r0_ = pl.multiple_of(t * 16, 16)
            ints = lbuf[pl.ds(r0_, 16), s].reshape(512, 256)
            full = lax.dot_general(ints, rounded, (((1,), (1,)), ((), ())), preferred_element_type=F32)
            lgrp[s, pl.ds(r0_, 16), :] = jnp.sum(full.reshape(16, 32, 256) * same[None], axis=1)
            return carry

        lax.fori_loop(0, 4, body, 0)

    def ladder_lanes():
        group = lax.broadcasted_iota(jnp.int32, (256, 128), 0) // 32
        slot = lax.broadcasted_iota(jnp.int32, (256, 128), 1)
        pick = jnp.where(group == slot, 1.0, 0.0).astype(F32)
        lsum[...] = jnp.dot(
            lgrp[...].reshape(256, 256), pick, precision=lax.Precision.HIGHEST, preferred_element_type=F32
        ).reshape(4, 4, 2, 8, 128)
        for d in range(1, 8):
            xd = lax.rem(xpos + d // 2, 4)
            cd = lax.rem(core + d % 2, 2)
            pltpu.make_async_remote_copy(
                src_ref=lsum.at[lax.rem(xd, 2) * 2 + cd, :, xd // 2], dst_ref=lrecv_a.at[d - 1],
                send_sem=sl.at[0], recv_sem=ql.at[0], device_id=at(z, y, xd, cd), device_id_type=MESH,
            ).start()

    def arrivals(ref, n):
        return pltpu.make_async_remote_copy(
            src_ref=ref, dst_ref=ref, send_sem=sl.at[n], recv_sem=ql.at[n], device_id=plane[0], device_id_type=MESH
        )

    def ladder_plane():
        arrivals(lrecv_a, 0).wait_recv()
        lplane[...] = lsum[narrow, :, xh] + jnp.sum(lrecv_a[...], axis=0)
        for d in range(1, 16):
            pltpu.make_async_remote_copy(
                src_ref=lplane.at[lax.rem(z + d // 4, 4)], dst_ref=lrecv_b.at[d - 1],
                send_sem=sl.at[1], recv_sem=ql.at[1], device_id=plane[d - 1], device_id_type=MESH,
            ).start()

    def ladder_end():
        arrivals(lrecv_b, 1).wait_recv()
        total = lplane[z] + jnp.sum(lrecv_b[...], axis=0)
        row = lax.broadcasted_iota(jnp.int32, (8, 128), 0)
        return [jnp.sum(jnp.where(row == 2 * y + e, total, 0.0), axis=0, keepdims=True) for e in range(2)]

    def fold(x):
        eight = jnp.sum(x.reshape(4, 8, 256), axis=0)
        return eight[:, :128] + eight[:, 128:]

    def tail(cls, ladder_rows, sums):
        row = lax.broadcasted_iota(jnp.int32, (32, 256), 0)
        lane = lax.broadcasted_iota(jnp.int32, (32, 256), 1)
        lane1 = lax.broadcasted_iota(jnp.int32, (1, 128), 1)
        lanes = lax.broadcasted_iota(jnp.int32, (32, 128), 1)
        rows = lax.broadcasted_iota(jnp.int32, (32, 128), 0)
        block = vir[:, pl.ds(pl.multiple_of(wide // 4 * 128, 128), 128)]
        down = jnp.sum(jnp.where(lanes == lax.rem(wide, 4) * 32 + rows, block, 0.0), axis=1, keepdims=True)
        across = vir[:, pl.ds(pl.multiple_of(narrow * 256, 256), 256)]
        for j in (2 * cls, 2 * cls + 1):
            for i in range(NI):
                ij = i * NJ + j
                placed = jnp.zeros((32, 256), F32)
                for e in range(2):
                    one = jnp.sum(jnp.where(lane1 == ij, ladder_rows[e], 0.0), axis=1, keepdims=True)
                    placed = jnp.where((row == e) & (lane == 0), one, placed)
                denominator = down + across - of_ref[:, i : i + 1] - os_ref[:, j : j + 1]
                a = amp[i, j]
                v = itg[i, j]
                r = v + part[j, i, z, xh, y] + placed - denominator * a
                new = a + r / denominator
                both_ref[1, i, j] = r
                both_ref[0, i, j] = new
                terms = [new * v] + [his[h, i, j] * r for h in range(4)] + [r * r]
                sums = [s + fold(t) for s, t in zip(sums, terms)]
        return sums

    relayout(0, 0)
    loads["u"].wait()
    load_rest()
    product(0, 0, 0, 1)
    pl.semaphore_wait(barrier, len(plane + row_of_chips))
    m1_one(0)
    product(0, 0, 1, 1)
    m1_one(1)
    product(0, 0, 2)
    m1(1, 0)
    relayout(3, 0)
    product(3, 0, 2)
    first_pair()
    m2_up(1, 0)
    m2_down(1, 0)
    relayout(1, 1)
    product(1, 1, 0)
    m3_up(1, 0)
    m3_down(1, 0)
    product(1, 1, 2)
    m1(1, 1)
    m2_up(0, 0)
    relayout(2, 1)
    product(2, 1, 0)
    m2_down(0, 0)
    m2_up(1, 1)
    m2_down(1, 1)
    product(2, 1, 2)
    ring_end(1, 0)
    m1(1, 2)
    m3_up(0, 0)
    m3_down(0, 0)
    product(3, 0, 0)
    m3_up(1, 1)
    m3_down(1, 1)
    m2_up(0, 1)
    m2_down(0, 1)
    second_pair()
    ladder_part(0)
    ladder_part(1)
    m3_up(0, 1)
    m3_down(0, 1)
    ladder_part(2)
    ring_end(0, 0)
    m2_up(1, 2)
    m2_down(1, 2)
    ladder_part(3)
    ladder_lanes()
    m2_up(0, 2)
    m2_down(0, 2)
    ring_end(1, 1)
    m3_up(1, 2)
    m3_down(1, 2)
    first_pair_end()
    m1(1, 3)
    m1(1, 4)
    late0(1)
    ring_end(0, 1)
    m3_up(0, 2)
    m3_down(0, 2)
    late0(0)
    m2_up(0, 3)
    m2_down(0, 3)
    ring_end(1, 2)
    m2_up(1, 3)
    m2_down(1, 3)
    late1(1)
    ladder_plane()
    second_pair_end()
    m3_up(0, 3)
    m3_down(0, 3)
    m2_up(0, 4)
    m2_down(0, 4)
    m3_up(1, 3)
    m3_down(1, 3)
    m3_up(0, 4)
    m3_down(0, 4)
    ring_end(0, 2)
    late1(0)
    m2_up(1, 4)
    m2_down(1, 4)
    m3_up(1, 4)
    m3_down(1, 4)
    late2(1)
    late2(0)
    for name in ("itg", "his", "vir", "of", "os"):
        loads[name].wait()
    ring_end(1, 3)
    ring_end(0, 3)
    ring_end(0, 4)
    ring_end(1, 4)
    rows = ladder_end()
    late3(1)
    sums = tail(1, rows, [jnp.zeros((8, 128), F32)] * 6)
    late3(0)
    sums = tail(0, rows, sums)

    lane = lax.broadcasted_iota(jnp.int32, (1, 128), 1)
    mine = jnp.zeros((1, 128), F32)
    for n, s in enumerate(sums):
        one = jnp.sum(jnp.sum(s, axis=0, keepdims=True), axis=1, keepdims=True)
        mine = jnp.where(lane == n, one, mine)

    def totals():
        me = wide * 4 + narrow
        sums_a[me] = mine

        def spread(d, carry):
            peer = lax.rem(me + d, 128)
            pltpu.make_async_remote_copy(
                src_ref=sums_a.at[me], dst_ref=sums_a.at[me], send_sem=ss.at[0], recv_sem=qs.at[0],
                device_id={"wide": peer // 4, "narrow": lax.rem(peer, 4)}, device_id_type=MESH,
            ).start()
            return carry

        lax.fori_loop(1, 128, spread, 0)
        others = sums_a.at[pl.ds(0, 127)]
        arrived = pltpu.make_async_remote_copy(
            src_ref=others, dst_ref=others, send_sem=ss.at[0], recv_sem=qs.at[0], device_id=plane[0], device_id_type=MESH
        )
        arrived.wait_recv()
        tot_ref[...] = jnp.sum(sums_a[...], axis=0) * (1.0 / 8388608.0)
        arrived.wait_send()

    totals()
    arrivals(lrecv_a, 0).wait_send()
    arrivals(lrecv_b, 1).wait_send()
    all_sent()


def shards(amplitudes, cycle_amps, cycle_ints, ladder_ints, integrals, history, vir_energy, occ_first, occ_second):
    bf16 = jnp.bfloat16
    dma = pltpu.SemaphoreType.DMA
    block = pltpu.VMEM((2, NI, NJ, 32, 256), F32)
    vmem = pl.BlockSpec(memory_space=pltpu.VMEM)
    stacked, totals = pl.pallas_call(
        kernel,
        out_shape=(block, pltpu.VMEM((1, 128), F32)),
        in_specs=[pl.BlockSpec(memory_space=pltpu.HBM)] * 9,
        out_specs=(vmem, vmem),
        scratch_shapes=[
            pltpu.VMEM((4, DEPTH, 4, 256), bf16),
            pltpu.VMEM((NI, DEPTH, 256), bf16),
            pltpu.VMEM((2, 4, DEPTH, 256), bf16),
            pltpu.VMEM((NJ, NI, 4, 2, 4, 32, 256), F32),
            pltpu.VMEM((2, 2, 2, 4, 32, 256), F32),
            pltpu.VMEM((2, 6, 4, 2, 2, 32, 256), F32),
            pltpu.VMEM((2, 4, 2, 2, 32, 256), F32),
            pltpu.VMEM((2, 4, 32, 256), F32),
            pltpu.VMEM((3, 2, 32, 256), F32),
            pltpu.VMEM((2, 6, 2, 32, 256), F32),
            pltpu.VMEM((64, 4, 32, 256), bf16),
            pltpu.VMEM((4, 64, 256), F32),
            pltpu.VMEM((4, 4, 2, 8, 128), F32),
            pltpu.VMEM((7, 4, 8, 128), F32),
            pltpu.VMEM((4, 8, 128), F32),
            pltpu.VMEM((15, 8, 128), F32),
            pltpu.VMEM((NI, NJ, 32, 256), F32),
            pltpu.VMEM((NI, NJ, 32, 256), F32),
            pltpu.VMEM((4, NI, NJ, 32, 256), F32),
            pltpu.VMEM((1, 1024), F32),
            pltpu.VMEM((1, NI), F32),
            pltpu.VMEM((1, NJ), F32),
            pltpu.VMEM((128, 1, 128), F32),
            dma((17,)),
            dma((15,)),
            dma((2,)),
            dma((2, 5)),
            dma((2, 5)),
            dma((2, 5)),
            dma((2, 3)),
            dma((2,)),
            dma((2,)), dma((2,)),
            dma((1,)), dma((1,)),
        ],
        compiler_params=pltpu.CompilerParams(
            collective_id=0, has_side_effects=True, vmem_limit_bytes=52 * 2**20
        ),
        cost_estimate=pl.CostEstimate(flops=9 * 10**9, bytes_accessed=27 * 10**6, transcendentals=0),
        name="window",
    )(*(pltpu.with_memory_space_constraint(x, pltpu.HBM) for x in (
        amplitudes,
        cycle_amps.reshape(NI, DEPTH, 256),
        cycle_ints.reshape(DEPTH, 4, 1024),
        ladder_ints,
        integrals,
        history,
        vir_energy.reshape(1, 1024),
        occ_first.reshape(1, NI),
        occ_second.reshape(1, NJ),
    )))
    return stacked[0], stacked[1], totals[0, :1], totals[0, 1:6]


def solution(mesh):
    spread = P(None, None, "wide", "narrow")
    return jax.shard_map(
        shards,
        mesh=mesh,
        in_specs=(
            spread,
            spread,
            P(None, "wide", None, None),
            spread,
            spread,
            P(None, None, None, "wide", "narrow"),
            P(),
            P(),
            P(),
        ),
        out_specs=(spread, spread, P(), P()),
        check_vma=False,
    )
```
